32 devices in a mesh: grp: 4 (over y, x), blk: 8 (over z, core).
Axes of the slice: x: 2, y: 2, z: 4, core: 2. Of those that a mesh axis runs over, the one named last changes fastest.
Arguments:
- integrals: float32 [48, 1024, 1536], P('grp', 'blk'), may hold values from -0.9 to 0.9
- pair_lists: int32 [4, 2], P('grp'), may hold values from 0 to 48, as said below
- row_orbital: int32 [48], P('grp'), may hold values from 0 to 47, each once
- occ_energy: float32 [48], replicated, may hold values from -2 to -0.5
- vir_energy: float32 [1024], P('blk'), may hold values from 0.5 to 4
Outputs:
- three_index_density: float32 [48, 1024, 1536], P('grp', 'blk')
The draws below stay inside these ranges and needn't reach their ends.
Inputs may be any that keep to these rules, and one draw needn't show every extreme that they name: `pair_lists`: entries are rows of the integrals, or 48 in unused slots; used slots come first; every group lists one to 2 rows, some group exactly one and some exactly 2; no two rows listed by one group are held by the same group (a group may list one of its own rows). `row_orbital`: each orbital stands in exactly one row.
All inputs are finite; a program needn't handle non-finite values.
Results may differ from the reference program's by a relative error of at most 0.0001.
Values sent between devices are 32-bit elements; how exact they have to be, the bound alone decides.
No kernel may reach another device: no remote copies, remote signals or barrier semaphores. Data moves between devices by JAX's collectives and lax.ppermute only.
A program may use at most 128 MiB of HBM per device.

```python
import jax
import jax.numpy as jnp
from jax import lax

V = 1024
X = 1536
OCC_GRP = 12
MAXJ = 2
GROUPS = 4
O = 48


def draw_pair_lists(key, part):
    key_count, key_busy, key_owner, key_offset = jax.random.split(key, 4)
    counts = jax.random.randint(key_count, (GROUPS,), 1, MAXJ + 1)
    busiest = jax.random.randint(key_busy, (), 0, GROUPS)
    lightest = (busiest + 1) % GROUPS
    group_ids = jnp.arange(GROUPS)
    counts = jnp.where(group_ids == busiest, MAXJ, counts)
    counts = jnp.where(group_ids == lightest, 1, counts)
    owner_keys = jax.random.split(key_owner, GROUPS)
    owners = jax.vmap(lambda owner_key: jax.random.permutation(owner_key, GROUPS))(owner_keys)[:, :MAXJ]
    offsets = jax.random.randint(key_offset, (GROUPS, MAXJ), 0, OCC_GRP)
    listed = owners * OCC_GRP + offsets
    slot_grid = jnp.arange(MAXJ)[None, :]
    return jnp.where(slot_grid < counts[:, None], listed, O).astype(jnp.int32)


def level_of(key, dims, shards, smallest, high):
    def one(position, parts):
        draws = jax.random.uniform(jax.random.fold_in(jax.random.fold_in(key, 6), position), (parts,), jnp.float32, smallest / len(shards), high / len(shards))
        return jnp.repeat(jnp.exp(draws), dims[position] // parts).reshape((-1,) + (1,) * (len(dims) - position - 1))

    loudness = one(*shards[0])
    for cut in shards[1:]:
        loudness = loudness * one(*cut)
    return loudness


def normal_values(stream_key, dims, deviation, limit, shards=(), held_as=jnp.bfloat16):
    array = deviation * jax.random.normal(stream_key, dims, jnp.float32)
    if shards:
        array = array * level_of(stream_key, dims, shards, -0.22, 0.18)
    return jnp.clip(array, -limit, limit).astype(held_as)


def setup_inputs(seed: int = 0) -> dict:
    key_list = jax.random.split(jax.random.key(seed), 6)
    return {
        "integrals": normal_values(key_list[0], (O, V, X), 0.15, 0.9, ((0, 4), (1, 8)), jnp.float32),
        "pair_lists": draw_pair_lists(jax.random.fold_in(key_list[5], 71), 0),
        "row_orbital": jax.random.permutation(key_list[2], O).astype(jnp.int32),
        "occ_energy": jnp.clip(jax.random.uniform(key_list[3], (O,), jnp.float32, -2.0, -0.5), -2.0, -0.5),
        "vir_energy": jnp.clip(0.5 + 3.5 * jax.random.uniform(key_list[4], (V,), jnp.float32) ** level_of(key_list[4], (V,), ((0, 8),), -0.2, 0.2), 0.5, 4.0),
    }


def reference(integrals, pair_lists, row_orbital, occ_energy, vir_energy):
    highest = lax.Precision.HIGHEST
    density = jnp.zeros(integrals.shape, jnp.float32)
    row_energy = occ_energy[row_orbital]
    for group_index in range(GROUPS):
        first_row = group_index * OCC_GRP
        own_rows = integrals[first_row:first_row + OCC_GRP]
        own_energy = row_energy[first_row:first_row + OCC_GRP]
        for slot_index in range(MAXJ):
            target = pair_lists[group_index, slot_index]
            is_valid = (target < O).astype(jnp.float32)
            row_index = jnp.minimum(target, O - 1).astype(jnp.int32)
            partner = lax.dynamic_index_in_dim(integrals, row_index, 0, keepdims=False) * is_valid
            pair_block = jnp.einsum('iap,bp->iab', own_rows, partner, precision=highest)
            denominator = (own_energy[:, None, None] + row_energy[row_index]
                           - vir_energy[None, :, None] - vir_energy[None, None, :])
            amplitude = pair_block / denominator
            forward = jnp.einsum('iab,bp->iap', amplitude, partner, precision=highest)
            density = density.at[first_row:first_row + OCC_GRP].add(forward)
            returned = jnp.einsum('iab,iap->bp', amplitude, own_rows, precision=highest)
            current = lax.dynamic_index_in_dim(density, row_index, 0, keepdims=False)
            density = lax.dynamic_update_index_in_dim(density, current + returned * is_valid, row_index, 0)
    return density
```

```python
import functools

import jax
import jax.numpy as jnp
from jax import lax
from jax.experimental import pallas as pl
from jax.experimental.pallas import tpu as pltpu
from jax.sharding import PartitionSpec as P

PIECES = 2
CORES = 2
VMEM = 56 * 1024 * 1024


def split(x):
    high = x.astype(jnp.bfloat16)
    return high, (x - high.astype(jnp.float32)).astype(jnp.bfloat16)


def dot(a, b, contract):
    return lax.dot_general(a, b, ((contract[:1], contract[1:]), ((), ())), preferred_element_type=jnp.float32)


def block_rows(total, most):
    rows = most
    while total % rows:
        rows //= 2
    return rows


def split_kernel(x_ref, high_ref, low_ref):
    high, low = split(x_ref[...])
    high_ref[...] = high
    low_ref[...] = low


def split_rows(x):
    rows, width = x.shape
    step = block_rows(rows, 256)
    spec = pl.BlockSpec((step, width), lambda i: (i, 0))
    half = jax.ShapeDtypeStruct(x.shape, jnp.bfloat16)
    return pl.pallas_call(
        split_kernel,
        grid=(rows // step,),
        in_specs=[spec],
        out_specs=[spec, spec],
        out_shape=[half, half],
        cost_estimate=pl.CostEstimate(flops=2 * rows * width, bytes_accessed=8 * rows * width, transcendentals=0),
        compiler_params=pltpu.CompilerParams(vmem_limit_bytes=VMEM),
    )(x)


def unit_kernel(steps, chip_ref, own_high, own_low, sib_high, sib_low, row_ref, col_ref, *refs):
    parts = refs[:PIECES]
    t_high, t_low, r_high, r_low = refs[PIECES:PIECES + 4]
    grads = refs[PIECES + 4:2 * PIECES + 4]
    step = pl.program_id(0)
    width = parts[0].shape[0]

    @pl.when(step == 0)
    def _():
        for p in range(PIECES):
            high, low = split(parts[p][...])
            r_high[p * width:(p + 1) * width] = high
            r_low[p * width:(p + 1) * width] = low
            grads[p][...] = jnp.zeros_like(grads[p])

    def work(a_high_ref, a_low_ref):
        a_high = a_high_ref[...]
        a_low = a_low_ref[...]
        high, low = r_high[...], r_low[...]
        pair = dot(a_high, high, (1, 1)) + dot(a_high, low, (1, 1)) + dot(a_low, high, (1, 1))
        amplitude = pair / (row_ref[...] + col_ref[0])
        up, down = split(amplitude)
        t_high[...] = up
        t_low[...] = down
        up, down = split(amplitude.T)
        for p in range(PIECES):
            part = slice(p * width, (p + 1) * width)
            grads[p][...] += (
                dot(up[part], a_high, (1, 0)) + dot(down[part], a_high, (1, 0)) + dot(up[part], a_low, (1, 0))
            )

    @pl.when(step < steps)
    def _():
        work(own_high, own_low)

    @pl.when(step >= steps)
    def _():
        work(sib_high, sib_low)


def unit(chip, halves, row_energy, col_energy, parts):
    (own_high, own_low), (sib_high, sib_low) = halves
    rows, aux = own_high.shape
    step = block_rows(rows, 512)
    steps = rows // step
    part_rows = parts[0].shape[0]
    cols = part_rows * PIECES
    own = pl.BlockSpec((step, aux), lambda i, c: (jnp.minimum(i, steps - 1), 0))
    sib = pl.BlockSpec((step, aux), lambda i, c: (jnp.maximum(i - steps, 0), 0))
    whole = lambda shape: pl.BlockSpec(shape, lambda i, c: (0, 0))
    bf16 = lambda *shape: jax.ShapeDtypeStruct(shape, jnp.bfloat16)
    t_spec = pl.BlockSpec((step, cols), lambda i, c: (i, 0))
    outs = pl.pallas_call(
        functools.partial(unit_kernel, steps),
        grid_spec=pltpu.PrefetchScalarGridSpec(
            num_scalar_prefetch=1,
            grid=(2 * steps,),
            in_specs=[
                own, own, sib, sib,
                pl.BlockSpec((step, 1), lambda i, c: (i, 0)),
                pl.BlockSpec((1, 1, cols), lambda i, c: (c[0], 0, 0)),
            ] + [whole((part_rows, aux))] * PIECES,
            out_specs=[t_spec, t_spec, whole((cols, aux)), whole((cols, aux))] + [whole((part_rows, aux))] * PIECES,
        ),
        out_shape=[bf16(2 * rows, cols)] * 2 + [bf16(cols, aux)] * 2
        + [jax.ShapeDtypeStruct((part_rows, aux), jnp.float32)] * PIECES,
        cost_estimate=pl.CostEstimate(
            flops=24 * rows * aux * cols, bytes_accessed=8 * rows * aux + 16 * cols * aux, transcendentals=0
        ),
        compiler_params=pltpu.CompilerParams(vmem_limit_bytes=VMEM),
    )(chip, own_high, own_low, sib_high, sib_low, row_energy, col_energy, *parts)
    return outs[:4], outs[4:]


def forward_kernel(count, *refs):
    start = refs[:-1][4 * count:]
    total = start[0][...] if start else None
    for u in range(count):
        t_high, t_low, r_high, r_low = (ref[...] for ref in refs[4 * u:4 * u + 4])
        term = dot(t_high, r_high, (1, 0)) + dot(t_high, r_low, (1, 0)) + dot(t_low, r_high, (1, 0))
        total = term if total is None else total + term
    refs[-1][...] = total


def forward(half, units, start):
    rows = units[0][0].shape[0] // 2
    cols, aux = units[0][2].shape
    step = block_rows(rows, 256)
    steps = rows // step
    t_spec = pl.BlockSpec((step, cols), lambda i: (i + half * steps, 0))
    r_spec = pl.BlockSpec((cols, aux), lambda i: (0, 0))
    out_spec = pl.BlockSpec((step, aux), lambda i: (i, 0))
    operands = [x for one in units for x in one] + ([] if start is None else [start])
    return pl.pallas_call(
        functools.partial(forward_kernel, len(units)),
        grid=(steps,),
        in_specs=[t_spec, t_spec, r_spec, r_spec] * len(units) + [out_spec] * (start is not None),
        out_specs=out_spec,
        out_shape=jax.ShapeDtypeStruct((rows, aux), jnp.float32),
        cost_estimate=pl.CostEstimate(
            flops=6 * rows * aux * cols * len(units), bytes_accessed=8 * rows * aux, transcendentals=0
        ),
        compiler_params=pltpu.CompilerParams(vmem_limit_bytes=VMEM),
    )(*operands)


def ring_order(chips):
    return [0] + list(range(1, chips, 2)) + [z for z in range(chips - 1, 0, -1) if z % 2 == 0]


def body(integrals, pair_lists, row_orbital, occ_energy, vir_energy):
    own_count, width, aux = integrals.shape
    slots = pair_lists.shape[1]
    groups = lax.axis_size("grp")
    me = lax.axis_index("grp")
    place = lax.axis_index("blk")
    chips = lax.axis_size("blk") // CORES
    core = lax.rem(place, CORES)
    chip = lax.div(place, CORES)
    order = ring_order(chips)
    pairs = [
        (order[i] * CORES + c, order[(i + 1) % chips] * CORES + c) for i in range(chips) for c in range(CORES)
    ]
    swap = [(i, i ^ 1) for i in range(chips * CORES)]
    hop = lambda x: lax.ppermute(x, "blk", pairs)
    sibling = lambda x: lax.ppermute(x, "blk", swap)
    to_group = lambda x, k: lax.ppermute(x, "grp", [(g, g ^ k) for g in range(groups)])

    own_rows = integrals.reshape(own_count * width, aux)
    sib_rows = sibling(own_rows)

    picks = row_orbital[:, None] == lax.broadcasted_iota(jnp.int32, (own_count, occ_energy.shape[0]), 1)
    own_energy = jnp.sum(jnp.where(picks, occ_energy[None, :], 0.0), axis=1)
    packet = jnp.concatenate([pair_lists[0].astype(jnp.float32), own_energy])
    table = lax.all_gather(packet, "grp", axis=0)
    listed = table[:, :slots].astype(jnp.int32)
    row_energies = table[:, slots:].reshape(-1)
    holder = lax.div(listed, own_count)
    local = listed - holder * own_count
    mine = holder[me]

    rows_for = []
    asked_by = []
    for k in range(groups):
        asks = holder[me ^ k] == me
        asked_by.append(jnp.any(asks))
        rows_for.append(jnp.sum(jnp.where(asks, local[me ^ k], 0)))
    part_width = width // PIECES
    partners = []
    for p in range(PIECES):
        got = []
        for k in range(groups):
            block = lax.dynamic_slice(integrals, (rows_for[k], p * part_width, 0), (1, part_width, aux))[0]
            got.append(to_group(block, k) if k else block)
        chosen = []
        for s in range(slots):
            one = jnp.zeros((part_width, aux), jnp.float32)
            for k in range(groups):
                one = jnp.where(mine[s] == me ^ k, got[k], one)
            chosen.append(one)
        partners.append(jnp.concatenate(chosen, axis=0))

    virtual = lax.all_gather(vir_energy, "blk", axis=0)
    virtual = lax.dynamic_index_in_dim(virtual.reshape(chips, CORES, width), core, 1, keepdims=False)
    row_ids = lax.broadcasted_iota(jnp.int32, (slots, row_energies.shape[0]), 1)
    partner_energy = jnp.sum(jnp.where(listed[me][:, None] == row_ids, row_energies[None, :], 0.0), axis=1)
    col_energy = partner_energy[None, None, :, None] - virtual.reshape(chips, PIECES, 1, part_width)
    col_energy = col_energy.reshape(chips, 1, slots * width)
    sib_virtual = sibling(vir_energy)
    row_energy = own_energy[None, :, None] - jnp.stack([vir_energy, sib_virtual])[:, None, :]
    row_energy = row_energy.reshape(CORES * own_count * width, 1)

    halves = (split_rows(own_rows), split_rows(sib_rows))
    spot = sum(jnp.where(chip == z, i, 0) for i, z in enumerate(order))
    chip_at = lambda i: sum(jnp.where(i == j, z, 0) for j, z in enumerate(order))

    units = []
    grads = []
    parts = partners
    for s in range(chips):
        source = chip_at(lax.rem(spot - s + chips, chips)).astype(jnp.int32).reshape(1)
        one, grad = unit(source, halves, row_energy, col_energy, parts)
        units.append(one)
        grads.append(grad)
        if s < chips - 1:
            parts = [hop(x) for x in parts]

    shares = []
    for p in range(PIECES):
        total = grads[1][p]
        for s in range(2, chips + 1):
            total = hop(total) + grads[s % chips][p]
        shares.append(total.reshape(slots, part_width, aux))

    away = sibling(forward(1, units, None))
    density = forward(0, units, away).reshape(own_count, width, aux)
    for p in range(PIECES):
        for k in range(groups):
            back = jnp.zeros((part_width, aux), jnp.float32)
            for s in range(slots):
                back = jnp.where(mine[s] == me ^ k, shares[p][s], back)
            back = to_group(back, k) if k else back
            spot_of = (rows_for[k], p * part_width, 0)
            old = lax.dynamic_slice(density, spot_of, (1, part_width, aux))
            new = old + jnp.where(asked_by[k], back, 0.0)[None]
            density = lax.dynamic_update_slice(density, new, spot_of)
    return density


def solution(mesh):
    in_specs = (P("grp", "blk", None), P("grp", None), P("grp"), P(), P("blk"))
    out_specs = P("grp", "blk", None)
    return jax.shard_map(body, mesh=mesh, in_specs=in_specs, out_specs=out_specs, check_vma=False)
```

```python
import functools

import jax
import jax.numpy as jnp
from jax import lax
from jax.experimental import pallas as pl
from jax.experimental.pallas import tpu as pltpu
from jax.sharding import PartitionSpec as P

PIECES = 2
CORES = 2
SCALE = 1
VMEM = 56 * 1024 * 1024
ANY = pl.BlockSpec(memory_space=pl.ANY)
SMEM = pl.BlockSpec(memory_space=pltpu.SMEM)
LOCAL = pl.BlockSpec(memory_space=pltpu.VMEM)
PARAMS = pltpu.CompilerParams(vmem_limit_bytes=VMEM)


def split(x):
    high = x.astype(jnp.bfloat16)
    return high, (x - high.astype(jnp.float32)).astype(jnp.bfloat16)


def dot(a, b, contract):
    return lax.dot_general(a, b, ((contract[:1], contract[1:]), ((), ())), preferred_element_type=jnp.float32)


def block_rows(total, most):
    rows = most
    while total % rows:
        rows //= 2
    return rows


def after(x, *others):
    return lax.optimization_barrier((x, others))[0]


def cost(flops, moved):
    return pl.CostEstimate(flops=flops // SCALE, bytes_accessed=moved // SCALE, transcendentals=0)


def split_kernel(x_ref, high_ref, low_ref):
    high_ref[...], low_ref[...] = split(x_ref[...])


def split_rows(x):
    rows, width = x.shape
    step = block_rows(rows, 256)
    spec = pl.BlockSpec((step, width), lambda i: (i, 0))
    half = jax.ShapeDtypeStruct(x.shape, jnp.bfloat16)
    return pl.pallas_call(
        split_kernel,
        grid=(rows // step,),
        in_specs=[spec],
        out_specs=[spec, spec],
        out_shape=[half, half],
        cost_estimate=cost(2 * rows * width, 8 * rows * width),
        compiler_params=PARAMS,
    )(x)


def asked_row(lists, me, slots, own_count):
    asked, row = False, 0
    for s in range(slots):
        entry = lists[s]
        hit = lax.div(entry, own_count) == me
        asked = jnp.logical_or(asked, hit)
        row = jnp.where(hit, entry - me * own_count, row)
    return asked, row


def slot_holder(lists, me, s, own_count):
    return lax.bitwise_xor(lax.div(lists[s], own_count), me)


def pick_kernel(groups, slots, own_count, first, me_ref, *refs):
    lists, x_ref, outs, sem = refs[:groups], refs[groups], refs[groups + 1:-1], refs[-1]
    rows = outs[0].shape[0]
    copies = []
    for k in range(1, groups):
        _, row = asked_row(lists[k], me_ref[0], slots, own_count)
        copies.append(pltpu.make_async_copy(x_ref.at[row, pl.ds(first, rows)], outs[k - 1], sem.at[k - 1]))
        copies[-1].start()
    for copy in copies:
        copy.wait()


def pick(me, lists, slots, integrals, first, rows):
    own_count, _, aux = integrals.shape
    groups = len(lists)
    return pl.pallas_call(
        functools.partial(pick_kernel, groups, slots, own_count, first),
        in_specs=[SMEM] * (groups + 1) + [ANY],
        out_specs=[LOCAL] * (groups - 1),
        out_shape=[jax.ShapeDtypeStruct((rows, aux), jnp.float32)] * (groups - 1),
        scratch_shapes=[pltpu.SemaphoreType.DMA((groups - 1,))],
        cost_estimate=cost(0, 8 * rows * aux * groups),
        compiler_params=PARAMS,
    )(me, *lists, integrals)


def choose_kernel(groups, slots, own_count, first, me_ref, lists, x_ref, *refs):
    got, out, sem = refs[:groups - 1], refs[groups - 1], refs[groups]
    rows = out.shape[0] // slots
    me = me_ref[0]
    for s in range(slots):
        k_of = slot_holder(lists, me, s, own_count)
        to = out.at[pl.ds(s * rows, rows)]
        row = jnp.clip(lists[s] - me * own_count, 0, own_count - 1)

        @pl.when(k_of == 0)
        def _():
            pltpu.make_async_copy(x_ref.at[row, pl.ds(first, rows)], to, sem.at[s]).start()

        for k in range(1, groups):
            @pl.when(k_of == k)
            def _():
                pltpu.make_async_copy(got[k - 1], to, sem.at[s]).start()

        @pl.when(k_of >= groups)
        def _():
            to[...] = jnp.zeros_like(to)

    for s in range(slots):
        @pl.when(slot_holder(lists, me, s, own_count) < groups)
        def _():
            pltpu.make_async_copy(got[0], out.at[pl.ds(s * rows, rows)], sem.at[s]).wait()


def choose(me, lists, slots, integrals, got, first):
    own_count, _, aux = integrals.shape
    rows = got[0].shape[0]
    groups = len(got) + 1
    return pl.pallas_call(
        functools.partial(choose_kernel, groups, slots, own_count, first),
        in_specs=[SMEM, SMEM] + [ANY] * groups,
        out_specs=LOCAL,
        out_shape=jax.ShapeDtypeStruct((slots * rows, aux), jnp.float32),
        scratch_shapes=[pltpu.SemaphoreType.DMA((slots,))],
        cost_estimate=cost(0, 8 * rows * aux * slots),
        compiler_params=PARAMS,
    )(me, lists, integrals, *got)


def back_kernel(groups, slots, own_count, me_ref, lists, share, *refs):
    outs, sem = refs[:-1], refs[-1]
    rows = outs[0].shape[0]
    copies = []
    for k in range(1, groups):
        slot = 0
        for s in range(slots):
            slot = jnp.where(slot_holder(lists, me_ref[0], s, own_count) == k, s, slot)
        start = pl.multiple_of(slot * rows, rows)
        copies.append(pltpu.make_async_copy(share.at[pl.ds(start, rows)], outs[k - 1], sem.at[k - 1]))
        copies[-1].start()
    for copy in copies:
        copy.wait()


def back(me, lists, slots, own_count, share, groups):
    rows, aux = share.shape[0] // slots, share.shape[1]
    return pl.pallas_call(
        functools.partial(back_kernel, groups, slots, own_count),
        in_specs=[SMEM, SMEM, ANY],
        out_specs=[LOCAL] * (groups - 1),
        out_shape=[jax.ShapeDtypeStruct((rows, aux), jnp.float32)] * (groups - 1),
        scratch_shapes=[pltpu.SemaphoreType.DMA((groups - 1,))],
        cost_estimate=cost(0, 8 * rows * aux * groups),
        compiler_params=PARAMS,
    )(me, lists, share)


def finish_kernel(groups, slots, own_count, first, me_ref, *refs):
    lists, share, arrived = refs[:groups], refs[groups], refs[groups + 1:2 * groups]
    _, density, held, added, sem_held, sem_added = refs[2 * groups:]
    rows = held.shape[1]
    me = me_ref[0]
    asked, places, heads = [], [], []
    for k in range(groups):
        is_asked, row = asked_row(lists[k], me, slots, own_count)
        head = k
        for j in range(k - 1, -1, -1):
            head = jnp.where(jnp.logical_and(asked[j], places[j] == row), j, head)
        asked.append(is_asked)
        places.append(row)
        heads.append(head)
    slot = 0
    for s in range(slots):
        slot = jnp.where(slot_holder(lists[0], me, s, own_count) == 0, s, slot)
    start = pl.multiple_of(slot * rows, rows)
    leads = [jnp.logical_and(asked[k], heads[k] == k) for k in range(groups)]
    source = [share.at[pl.ds(start, rows)]] + list(arrived)
    spots = [density.at[places[k], pl.ds(first, rows)] for k in range(groups)]
    reads = [pltpu.make_async_copy(spots[k], held.at[k], sem_held.at[k]) for k in range(groups)]
    terms = [pltpu.make_async_copy(source[k], added.at[k], sem_added.at[k]) for k in range(groups)]
    writes = [pltpu.make_async_copy(held.at[k], spots[k], sem_held.at[k]) for k in range(groups)]
    for k in range(groups):
        pl.when(leads[k])(reads[k].start)
        pl.when(asked[k])(terms[k].start)
    for k in range(groups):
        pl.when(leads[k])(reads[k].wait)
    for k in range(groups):
        @pl.when(asked[k])
        def _():
            terms[k].wait()
            held[heads[k]] = held[heads[k]] + added[k]
    for k in range(groups):
        pl.when(leads[k])(writes[k].start)
    for k in range(groups):
        pl.when(leads[k])(writes[k].wait)


def finish(me, lists, slots, share, arrived, density, first):
    own_count, _, aux = density.shape
    groups = len(lists)
    rows = share.shape[0] // slots
    return pl.pallas_call(
        functools.partial(finish_kernel, groups, slots, own_count, first),
        in_specs=[SMEM] * (groups + 1) + [ANY] * (groups + 1),
        out_specs=ANY,
        out_shape=jax.ShapeDtypeStruct(density.shape, jnp.float32),
        input_output_aliases={2 * groups + 1: 0},
        scratch_shapes=[
            pltpu.VMEM((groups, rows, aux), jnp.float32),
            pltpu.VMEM((groups, rows, aux), jnp.float32),
            pltpu.SemaphoreType.DMA((groups,)),
            pltpu.SemaphoreType.DMA((groups,)),
        ],
        cost_estimate=cost(0, 12 * rows * aux * groups),
        compiler_params=PARAMS,
    )(me, *lists, share, *arrived, density)


def unit_kernel(steps, own_high, own_low, sib_high, sib_low, row_ref, col_ref, *refs):
    parts = refs[:PIECES]
    t_high, t_low, r_high, r_low = refs[PIECES:PIECES + 4]
    grads = refs[PIECES + 4:2 * PIECES + 4]
    step = pl.program_id(0)
    width = parts[0].shape[0]

    @pl.when(step == 0)
    def _():
        for p in range(PIECES):
            part = slice(p * width, (p + 1) * width)
            r_high[part], r_low[part] = split(parts[p][...])
            grads[p][...] = jnp.zeros_like(grads[p])

    def work(a_high, a_low):
        high, low = r_high[...], r_low[...]
        pair = dot(high, a_high[...], (1, 1)) + dot(low, a_high[...], (1, 1)) + dot(high, a_low[...], (1, 1))
        up, down = split(pair / (row_ref[...] + col_ref[...]))
        t_high[...] = up
        t_low[...] = down
        term = dot(up, a_high[...], (1, 0)) + dot(down, a_high[...], (1, 0)) + dot(up, a_low[...], (1, 0))
        for p in range(PIECES):
            grads[p][...] += term[p * width:(p + 1) * width]

    @pl.when(step < steps)
    def _():
        work(own_high, own_low)

    @pl.when(step >= steps)
    def _():
        work(sib_high, sib_low)


def unit(halves, row_energy, col_energy, parts):
    (own_high, own_low), (sib_high, sib_low) = halves
    rows, aux = own_high.shape
    step = block_rows(rows, 512)
    steps = rows // step
    part_rows = parts[0].shape[0]
    cols = part_rows * PIECES
    own = pl.BlockSpec((step, aux), lambda i: (jnp.minimum(i, steps - 1), 0))
    sib = pl.BlockSpec((step, aux), lambda i: (jnp.maximum(i - steps, 0), 0))
    whole = lambda shape: pl.BlockSpec(shape, lambda i: (0, 0))
    bf16 = lambda *shape: jax.ShapeDtypeStruct(shape, jnp.bfloat16)
    t_spec = pl.BlockSpec((cols, step), lambda i: (0, i))
    outs = pl.pallas_call(
        functools.partial(unit_kernel, steps),
        grid=(2 * steps,),
        in_specs=[own, own, sib, sib, pl.BlockSpec((1, step), lambda i: (0, i)), whole((cols, 1))]
        + [whole((part_rows, aux))] * PIECES,
        out_specs=[t_spec, t_spec, whole((cols, aux)), whole((cols, aux))] + [whole((part_rows, aux))] * PIECES,
        out_shape=[bf16(cols, 2 * rows)] * 2 + [bf16(cols, aux)] * 2
        + [jax.ShapeDtypeStruct((part_rows, aux), jnp.float32)] * PIECES,
        cost_estimate=cost(24 * rows * aux * cols, 8 * rows * aux + 16 * cols * aux),
        compiler_params=PARAMS,
    )(own_high, own_low, sib_high, sib_low, row_energy, col_energy, *parts)
    return outs[:4], outs[4:]


def forward_kernel(count, spans, *refs):
    out = refs[-1]
    total = None
    for u in range(count):
        t_high, t_low, r_high, r_low = (ref[...] for ref in refs[4 * u:4 * u + 4])
        term = dot(t_high, r_high, (0, 0)) + dot(t_high, r_low, (0, 0)) + dot(t_low, r_high, (0, 0))
        total = term if total is None else total + term
    out[...] = total
    step = pl.program_id(0)
    for (begin, end), start in zip(spans, refs[4 * count:-1]):
        @pl.when(jnp.logical_and(step >= begin, step < end))
        def _():
            out[...] += start[...]


def forward(units, first, count, starts):
    cols, aux = units[0][2].shape
    step = block_rows(count, 256)
    steps = count // step
    spans = [(begin // step, (begin + rows.shape[0]) // step) for begin, rows in starts]
    t_spec = pl.BlockSpec((cols, step), lambda i: (0, i + first // step))
    r_spec = pl.BlockSpec((cols, aux), lambda i: (0, 0))
    out_spec = pl.BlockSpec((step, aux), lambda i: (i, 0))
    start_spec = lambda begin, end: pl.BlockSpec((step, aux), lambda i: (jnp.clip(i, begin, end - 1) - begin, 0))
    return pl.pallas_call(
        functools.partial(forward_kernel, len(units), spans),
        grid=(steps,),
        in_specs=[t_spec, t_spec, r_spec, r_spec] * len(units) + [start_spec(*span) for span in spans],
        out_specs=out_spec,
        out_shape=jax.ShapeDtypeStruct((count, aux), jnp.float32),
        cost_estimate=cost(6 * count * aux * cols * len(units), 8 * count * aux),
        compiler_params=PARAMS,
    )(*(x for one in units for x in one), *(rows for _, rows in starts))


def ring_order(chips):
    return [0] + list(range(1, chips, 2)) + [z for z in range(chips - 1, 0, -1) if z % 2 == 0]


def body(integrals, pair_lists, row_orbital, occ_energy, vir_energy):
    own_count, width, aux = integrals.shape
    slots = pair_lists.shape[1]
    groups = lax.axis_size("grp")
    me = lax.axis_index("grp")
    me_ref = me.astype(jnp.int32).reshape(1)
    chips = lax.axis_size("blk") // CORES
    order = ring_order(chips)
    ring = lambda s: [
        (order[i] * CORES + c, order[(i + s) % chips] * CORES + c) for i in range(chips) for c in range(CORES)
    ]
    swap = [(i, i ^ 1) for i in range(chips * CORES)]
    along = lambda x, s: lax.ppermute(x, "blk", ring(s))
    hop = lambda x: along(x, 1)
    sibling = lambda x: lax.ppermute(x, "blk", swap)
    to_group = lambda x, k: lax.ppermute(x, "grp", [(g, g ^ k) for g in range(groups)])

    packet = jnp.concatenate([pair_lists[0], row_orbital])
    packets = [packet] + [to_group(packet, k) for k in range(1, groups)]
    own_rows = integrals.reshape(own_count * width, aux)
    sib_rows = sibling(own_rows)

    part_width = width // PIECES
    blocks = [pick(me_ref, packets, slots, integrals, p * part_width, part_width) for p in range(PIECES)]

    own_half = split_rows(after(own_rows, *blocks[-1]))

    ids = lax.broadcasted_iota(jnp.int32, (groups, own_count, occ_energy.shape[0]), 2)
    orbitals = jnp.stack(packets)[:, slots:]
    row_energies = jnp.sum(jnp.where(orbitals[:, :, None] == ids, occ_energy, 0.0), axis=2)
    held_rows = lax.bitwise_xor(lax.broadcasted_iota(jnp.int32, (groups, own_count), 0), me) * own_count
    held_rows = held_rows + lax.broadcasted_iota(jnp.int32, (groups, own_count), 1)
    listed_here = pair_lists[0][:, None, None] == held_rows
    partner_energy = jnp.sum(jnp.where(listed_here, row_energies, 0.0), axis=(1, 2))
    sib_virtual = sibling(vir_energy)
    row_energy = row_energies[0][None, :, None] - jnp.stack([vir_energy, sib_virtual])[:, None, :]
    row_energy = row_energy.reshape(1, CORES * own_count * width)
    virtual = jnp.stack([vir_energy] + [along(vir_energy, s) for s in range(1, chips)])
    col_energy = partner_energy[None, None, :, None] - virtual.reshape(chips, PIECES, 1, part_width)
    col_energy = list(col_energy.reshape(chips, slots * width, 1))

    pieces = []
    for p in range(PIECES):
        sent = after(blocks[p], *got) if p else blocks[p]
        got = [to_group(block, k + 1) for k, block in enumerate(sent)]
        if p == 1:
            halves = (own_half, split_rows(after(sib_rows, pieces[0][0])))
        got = after(got, halves, row_energy, col_energy, pieces[-1][0]) if p else after(got, own_half)
        part = choose(me_ref, packet, slots, integrals, got, p * part_width)
        pieces.append([part, hop(part)])
        if p == 1:
            pieces[0][1] = after(pieces[0][1], halves)
    parts = [piece[0] for piece in pieces]
    first = [piece[1] for piece in pieces]

    units = []
    grads = []
    for s in range(chips):
        if s == 1:
            parts = first
        elif s:
            parts = [hop(x) for x in parts]
        ready = list(parts)
        if s == 0:
            ready[1] = after(ready[1], first[0])
        if s == 1:
            ready = after(ready, *grads[0])
        if s == chips - 1:
            totals = [hop(after(grad, parts[0], *grads[-1])) for grad in grads[1]]
        one, grad = unit(halves, row_energy, col_energy[s], ready)
        units.append(one)
        grads.append(grad)
    rows = own_count * width
    tail = block_rows(rows, 256)
    head = rows - tail
    aside = []
    for s in range(2, chips + 1):
        done = totals
        if s == 2:
            totals[0] = after(totals[0], *grads[-1])
        totals = [x + y for x, y in zip(totals, grads[s % chips])]
        if s == 2:
            aside.append(forward(after(units, *done), rows, rows // 2, []))
        if s == chips - 1:
            aside.append(forward(after(units, *done), rows + rows // 2, rows // 2, []))
        if s < chips:
            totals = [hop(x) for x in totals]

    known = [(0, sibling(aside[0])), (rows // 2, sibling(aside[1]))]
    density = forward(units, 0, rows, known).reshape(own_count, width, aux)
    arrived = None
    for p in range(PIECES):
        sent = back(me_ref, packet, slots, own_count, after(totals[p], density), groups)
        if arrived is not None:
            sent = after(sent, *arrived)
        arrived = [to_group(block, k + 1) for k, block in enumerate(sent)]
        density = finish(me_ref, packets, slots, totals[p], arrived, density, p * part_width)
    return density


def solution(mesh):
    in_specs = (P("grp", "blk", None), P("grp", None), P("grp"), P(), P("blk"))
    out_specs = P("grp", "blk", None)
    return jax.shard_map(body, mesh=mesh, in_specs=in_specs, out_specs=out_specs, check_vma=False)
```

```python
import functools

import jax
import jax.numpy as jnp
from jax import lax
from jax.experimental import pallas as pl
from jax.experimental.pallas import tpu as pltpu
from jax.sharding import PartitionSpec as P

PIECES = 2
CORES = 2
SCALE = 1
VMEM = 56 * 1024 * 1024
ANY = pl.BlockSpec(memory_space=pl.ANY)
SMEM = pl.BlockSpec(memory_space=pltpu.SMEM)
LOCAL = pl.BlockSpec(memory_space=pltpu.VMEM)
PARAMS = pltpu.CompilerParams(vmem_limit_bytes=VMEM)


def split(x):
    high = x.astype(jnp.bfloat16)
    return high, (x - high.astype(jnp.float32)).astype(jnp.bfloat16)


def dot(a, b, contract):
    return lax.dot_general(a, b, ((contract[:1], contract[1:]), ((), ())), preferred_element_type=jnp.float32)


def block_rows(total, most):
    rows = most
    while total % rows:
        rows //= 2
    return rows


def after(x, *others):
    return lax.optimization_barrier((x, others))[0]


def cost(flops, moved):
    return pl.CostEstimate(flops=flops // SCALE, bytes_accessed=moved // SCALE, transcendentals=0)


def split_kernel(x_ref, high_ref, low_ref):
    high_ref[...], low_ref[...] = split(x_ref[...])


def split_rows(x):
    rows, width = x.shape
    step = block_rows(rows, 256)
    spec = pl.BlockSpec((step, width), lambda i: (i, 0))
    half = jax.ShapeDtypeStruct(x.shape, jnp.bfloat16)
    return pl.pallas_call(
        split_kernel,
        grid=(rows // step,),
        in_specs=[spec],
        out_specs=[spec, spec],
        out_shape=[half, half],
        cost_estimate=cost(2 * rows * width, 8 * rows * width),
        compiler_params=PARAMS,
    )(x)


def asked_row(lists, me, slots, own_count):
    asked, row = False, 0
    for s in range(slots):
        entry = lists[s]
        hit = lax.div(entry, own_count) == me
        asked = jnp.logical_or(asked, hit)
        row = jnp.where(hit, entry - me * own_count, row)
    return asked, row


def slot_holder(lists, me, s, own_count):
    return lax.bitwise_xor(lax.div(lists[s], own_count), me)


def pick_kernel(groups, slots, own_count, first, me_ref, *refs):
    lists, x_ref, outs, sem = refs[:groups], refs[groups], refs[groups + 1:-1], refs[-1]
    rows = outs[0].shape[0]
    copies = []
    for k in range(1, groups):
        _, row = asked_row(lists[k], me_ref[0], slots, own_count)
        copies.append(pltpu.make_async_copy(x_ref.at[row, pl.ds(first, rows)], outs[k - 1], sem.at[k - 1]))
        copies[-1].start()
    for copy in copies:
        copy.wait()


def pick(me, lists, slots, integrals, first, rows):
    own_count, _, aux = integrals.shape
    groups = len(lists)
    return pl.pallas_call(
        functools.partial(pick_kernel, groups, slots, own_count, first),
        in_specs=[SMEM] * (groups + 1) + [ANY],
        out_specs=[LOCAL] * (groups - 1),
        out_shape=[jax.ShapeDtypeStruct((rows, aux), jnp.float32)] * (groups - 1),
        scratch_shapes=[pltpu.SemaphoreType.DMA((groups - 1,))],
        cost_estimate=cost(0, 8 * rows * aux * groups),
        compiler_params=PARAMS,
    )(me, *lists, integrals)


def choose_kernel(groups, slots, own_count, first, me_ref, lists, x_ref, *refs):
    got, out, sem = refs[:groups - 1], refs[groups - 1], refs[groups]
    rows = out.shape[0] // slots
    me = me_ref[0]
    for s in range(slots):
        k_of = slot_holder(lists, me, s, own_count)
        to = out.at[pl.ds(s * rows, rows)]
        row = jnp.clip(lists[s] - me * own_count, 0, own_count - 1)

        @pl.when(k_of == 0)
        def _():
            pltpu.make_async_copy(x_ref.at[row, pl.ds(first, rows)], to, sem.at[s]).start()

        for k in range(1, groups):
            @pl.when(k_of == k)
            def _():
                pltpu.make_async_copy(got[k - 1], to, sem.at[s]).start()

        @pl.when(k_of >= groups)
        def _():
            to[...] = jnp.zeros_like(to)

    for s in range(slots):
        @pl.when(slot_holder(lists, me, s, own_count) < groups)
        def _():
            pltpu.make_async_copy(got[0], out.at[pl.ds(s * rows, rows)], sem.at[s]).wait()


def choose(me, lists, slots, integrals, got, first):
    own_count, _, aux = integrals.shape
    rows = got[0].shape[0]
    groups = len(got) + 1
    return pl.pallas_call(
        functools.partial(choose_kernel, groups, slots, own_count, first),
        in_specs=[SMEM, SMEM] + [ANY] * groups,
        out_specs=LOCAL,
        out_shape=jax.ShapeDtypeStruct((slots * rows, aux), jnp.float32),
        scratch_shapes=[pltpu.SemaphoreType.DMA((slots,))],
        cost_estimate=cost(0, 8 * rows * aux * slots),
        compiler_params=PARAMS,
    )(me, lists, integrals, *got)


def back_kernel(groups, slots, own_count, me_ref, lists, share, *refs):
    outs, sem = refs[:-1], refs[-1]
    rows = outs[0].shape[0]
    copies = []
    for k in range(1, groups):
        slot = 0
        for s in range(slots):
            slot = jnp.where(slot_holder(lists, me_ref[0], s, own_count) == k, s, slot)
        start = pl.multiple_of(slot * rows, rows)
        copies.append(pltpu.make_async_copy(share.at[pl.ds(start, rows)], outs[k - 1], sem.at[k - 1]))
        copies[-1].start()
    for copy in copies:
        copy.wait()


def back(me, lists, slots, own_count, share, groups):
    rows, aux = share.shape[0] // slots, share.shape[1]
    return pl.pallas_call(
        functools.partial(back_kernel, groups, slots, own_count),
        in_specs=[SMEM, SMEM, ANY],
        out_specs=[LOCAL] * (groups - 1),
        out_shape=[jax.ShapeDtypeStruct((rows, aux), jnp.float32)] * (groups - 1),
        scratch_shapes=[pltpu.SemaphoreType.DMA((groups - 1,))],
        cost_estimate=cost(0, 8 * rows * aux * groups),
        compiler_params=PARAMS,
    )(me, lists, share)


def finish_kernel(groups, slots, own_count, first, me_ref, *refs):
    lists, share, arrived = refs[:groups], refs[groups], refs[groups + 1:2 * groups]
    _, density, held, added, sem_held, sem_added = refs[2 * groups:]
    rows = held.shape[1]
    me = me_ref[0]
    asked, places, heads = [], [], []
    for k in range(groups):
        is_asked, row = asked_row(lists[k], me, slots, own_count)
        head = k
        for j in range(k - 1, -1, -1):
            head = jnp.where(jnp.logical_and(asked[j], places[j] == row), j, head)
        asked.append(is_asked)
        places.append(row)
        heads.append(head)
    slot = 0
    for s in range(slots):
        slot = jnp.where(slot_holder(lists[0], me, s, own_count) == 0, s, slot)
    start = pl.multiple_of(slot * rows, rows)
    leads = [jnp.logical_and(asked[k], heads[k] == k) for k in range(groups)]
    source = [share.at[pl.ds(start, rows)]] + list(arrived)
    spots = [density.at[places[k], pl.ds(first, rows)] for k in range(groups)]
    reads = [pltpu.make_async_copy(spots[k], held.at[k], sem_held.at[k]) for k in range(groups)]
    terms = [pltpu.make_async_copy(source[k], added.at[k], sem_added.at[k]) for k in range(groups)]
    writes = [pltpu.make_async_copy(held.at[k], spots[k], sem_held.at[k]) for k in range(groups)]
    for k in range(groups):
        pl.when(leads[k])(reads[k].start)
        pl.when(asked[k])(terms[k].start)
    for k in range(groups):
        pl.when(leads[k])(reads[k].wait)
    for k in range(groups):
        @pl.when(asked[k])
        def _():
            terms[k].wait()
            held[heads[k]] = held[heads[k]] + added[k]
    for k in range(groups):
        pl.when(leads[k])(writes[k].start)
    for k in range(groups):
        pl.when(leads[k])(writes[k].wait)


def finish(me, lists, slots, share, arrived, density, first):
    own_count, _, aux = density.shape
    groups = len(lists)
    rows = share.shape[0] // slots
    return pl.pallas_call(
        functools.partial(finish_kernel, groups, slots, own_count, first),
        in_specs=[SMEM] * (groups + 1) + [ANY] * (groups + 1),
        out_specs=ANY,
        out_shape=jax.ShapeDtypeStruct(density.shape, jnp.float32),
        input_output_aliases={2 * groups + 1: 0},
        scratch_shapes=[
            pltpu.VMEM((groups, rows, aux), jnp.float32),
            pltpu.VMEM((groups, rows, aux), jnp.float32),
            pltpu.SemaphoreType.DMA((groups,)),
            pltpu.SemaphoreType.DMA((groups,)),
        ],
        cost_estimate=cost(0, 12 * rows * aux * groups),
        compiler_params=PARAMS,
    )(me, *lists, share, *arrived, density)


def unit_kernel(steps, own_high, own_low, sib_high, sib_low, row_ref, col_ref, *refs):
    parts = refs[:PIECES]
    t_high, t_low, r_high, r_low = refs[PIECES:PIECES + 4]
    grads = refs[PIECES + 4:2 * PIECES + 4]
    step = pl.program_id(0)
    width = parts[0].shape[0]

    @pl.when(step == 0)
    def _():
        for p in range(PIECES):
            part = slice(p * width, (p + 1) * width)
            r_high[part], r_low[part] = split(parts[p][...])
            grads[p][...] = jnp.zeros_like(grads[p])

    def work(a_high, a_low):
        high, low = r_high[...], r_low[...]
        pair = dot(high, a_high[...], (1, 1)) + dot(low, a_high[...], (1, 1)) + dot(high, a_low[...], (1, 1))
        up, down = split(pair / (row_ref[...] + col_ref[...]))
        t_high[...] = up
        t_low[...] = down
        term = dot(up, a_high[...], (1, 0)) + dot(down, a_high[...], (1, 0)) + dot(up, a_low[...], (1, 0))
        for p in range(PIECES):
            grads[p][...] += term[p * width:(p + 1) * width]

    @pl.when(step < steps)
    def _():
        work(own_high, own_low)

    @pl.when(step >= steps)
    def _():
        work(sib_high, sib_low)


def unit(halves, row_energy, col_energy, parts):
    (own_high, own_low), (sib_high, sib_low) = halves
    rows, aux = own_high.shape
    step = block_rows(rows, 512)
    steps = rows // step
    part_rows = parts[0].shape[0]
    cols = part_rows * PIECES
    own = pl.BlockSpec((step, aux), lambda i: (jnp.minimum(i, steps - 1), 0))
    sib = pl.BlockSpec((step, aux), lambda i: (jnp.maximum(i - steps, 0), 0))
    whole = lambda shape: pl.BlockSpec(shape, lambda i: (0, 0))
    bf16 = lambda *shape: jax.ShapeDtypeStruct(shape, jnp.bfloat16)
    t_spec = pl.BlockSpec((cols, step), lambda i: (0, i))
    outs = pl.pallas_call(
        functools.partial(unit_kernel, steps),
        grid=(2 * steps,),
        in_specs=[own, own, sib, sib, pl.BlockSpec((1, step), lambda i: (0, i)), whole((cols, 1))]
        + [whole((part_rows, aux))] * PIECES,
        out_specs=[t_spec, t_spec, whole((cols, aux)), whole((cols, aux))] + [whole((part_rows, aux))] * PIECES,
        out_shape=[bf16(cols, 2 * rows)] * 2 + [bf16(cols, aux)] * 2
        + [jax.ShapeDtypeStruct((part_rows, aux), jnp.float32)] * PIECES,
        cost_estimate=cost(24 * rows * aux * cols, 8 * rows * aux + 16 * cols * aux),
        compiler_params=PARAMS,
    )(own_high, own_low, sib_high, sib_low, row_energy, col_energy, *parts)
    return outs[:4], outs[4:]


def forward_kernel(count, spans, *refs):
    out = refs[-1]
    total = None
    for u in range(count):
        t_high, t_low, r_high, r_low = (ref[...] for ref in refs[4 * u:4 * u + 4])
        term = dot(t_high, r_high, (0, 0)) + dot(t_high, r_low, (0, 0)) + dot(t_low, r_high, (0, 0))
        total = term if total is None else total + term
    out[...] = total
    step = pl.program_id(0)
    for (begin, end), start in zip(spans, refs[4 * count:-1]):
        @pl.when(jnp.logical_and(step >= begin, step < end))
        def _():
            out[...] += start[...]


def forward(units, first, count, starts):
    cols, aux = units[0][2].shape
    step = block_rows(count, 256)
    steps = count // step
    spans = [(begin // step, (begin + rows.shape[0]) // step) for begin, rows in starts]
    t_spec = pl.BlockSpec((cols, step), lambda i: (0, i + first // step))
    r_spec = pl.BlockSpec((cols, aux), lambda i: (0, 0))
    out_spec = pl.BlockSpec((step, aux), lambda i: (i, 0))
    start_spec = lambda begin, end: pl.BlockSpec((step, aux), lambda i: (jnp.clip(i, begin, end - 1) - begin, 0))
    return pl.pallas_call(
        functools.partial(forward_kernel, len(units), spans),
        grid=(steps,),
        in_specs=[t_spec, t_spec, r_spec, r_spec] * len(units) + [start_spec(*span) for span in spans],
        out_specs=out_spec,
        out_shape=jax.ShapeDtypeStruct((count, aux), jnp.float32),
        cost_estimate=cost(6 * count * aux * cols * len(units), 8 * count * aux),
        compiler_params=PARAMS,
    )(*(x for one in units for x in one), *(rows for _, rows in starts))


def ring_order(chips):
    return [0] + list(range(1, chips, 2)) + [z for z in range(chips - 1, 0, -1) if z % 2 == 0]


def body(integrals, pair_lists, row_orbital, occ_energy, vir_energy):
    own_count, width, aux = integrals.shape
    slots = pair_lists.shape[1]
    groups = lax.axis_size("grp")
    me = lax.axis_index("grp")
    me_ref = me.astype(jnp.int32).reshape(1)
    chips = lax.axis_size("blk") // CORES
    order = ring_order(chips)
    ring = lambda s: [
        (order[i] * CORES + c, order[(i + s) % chips] * CORES + c) for i in range(chips) for c in range(CORES)
    ]
    swap = [(i, i ^ 1) for i in range(chips * CORES)]
    along = lambda x, s: lax.ppermute(x, "blk", ring(s))
    hop = lambda x: along(x, 1)
    sibling = lambda x: lax.ppermute(x, "blk", swap)
    to_group = lambda x, k: lax.ppermute(x, "grp", [(g, g ^ k) for g in range(groups)])

    packet = jnp.concatenate([pair_lists[0], row_orbital])
    packets = [packet] + [to_group(packet, k) for k in range(1, groups)]
    own_rows = integrals.reshape(own_count * width, aux)
    sib_rows = sibling(own_rows)

    part_width = width // PIECES
    blocks = [pick(me_ref, packets, slots, integrals, p * part_width, part_width) for p in range(PIECES)]

    own_half = split_rows(after(own_rows, *blocks[-1]))

    ids = lax.broadcasted_iota(jnp.int32, (groups, own_count, occ_energy.shape[0]), 2)
    orbitals = jnp.stack(packets)[:, slots:]
    row_energies = jnp.sum(jnp.where(orbitals[:, :, None] == ids, occ_energy, 0.0), axis=2)
    held_rows = lax.bitwise_xor(lax.broadcasted_iota(jnp.int32, (groups, own_count), 0), me) * own_count
    held_rows = held_rows + lax.broadcasted_iota(jnp.int32, (groups, own_count), 1)
    listed_here = pair_lists[0][:, None, None] == held_rows
    partner_energy = jnp.sum(jnp.where(listed_here, row_energies, 0.0), axis=(1, 2))
    sib_virtual = sibling(vir_energy)
    row_energy = row_energies[0][None, :, None] - jnp.stack([vir_energy, sib_virtual])[:, None, :]
    row_energy = row_energy.reshape(1, CORES * own_count * width)
    virtual = jnp.stack([vir_energy] + [along(vir_energy, s) for s in range(1, chips)])
    col_energy = partner_energy[None, None, :, None] - virtual.reshape(chips, PIECES, 1, part_width)
    col_energy = list(col_energy.reshape(chips, slots * width, 1))

    pieces = []
    for p in range(PIECES):
        sent = blocks[p]
        got = [to_group(block, k + 1) for k, block in enumerate(sent)]
        if p == 1:
            halves = (own_half, split_rows(after(sib_rows, pieces[0][0])))
        got = after(got, halves, row_energy, col_energy, pieces[-1][0]) if p else after(got, own_half)
        part = choose(me_ref, packet, slots, integrals, got, p * part_width)
        pieces.append([part, hop(part)])
        if p == 1:
            pieces[0][1] = after(pieces[0][1], halves)
    parts = [piece[0] for piece in pieces]
    first = [piece[1] for piece in pieces]

    units = []
    grads = []
    for s in range(chips):
        if s == 1:
            parts = first
        elif s:
            parts = [hop(x) for x in parts]
        ready = list(parts)
        if s == 0:
            ready[1] = after(ready[1], first[0])
        if s == 1:
            ready = after(ready, *grads[0])
        if s == chips - 1:
            totals = [hop(after(grad, parts[0], *grads[-1])) for grad in grads[1]]
        one, grad = unit(halves, row_energy, col_energy[s], ready)
        units.append(one)
        grads.append(grad)
    rows = own_count * width
    step = block_rows(rows, 256)
    last = rows - step
    middle = 0
    last = rows // 2
    cuts = [(0, last), (last, rows)]
    aside = []
    for s in range(2, chips + 1):
        done = totals
        if s == 2:
            totals[0] = after(totals[0], *grads[-1])
        totals = [x + y for x, y in zip(totals, grads[s % chips])]
        if s == 2:
            aside.append(forward(after(units, *done), rows, last, []))
        if s == chips - 1:
            most = forward(after(units[:-1], done[0], aside[0]), rows + last, rows - last, [])
            ready = after(units, most, *done)
            aside.append(forward(ready[-1:], rows + last, rows - last, [(0, most)]))
        if s < chips:
            totals = [hop(x) for x in totals]

    early = forward(after(units[:-1], aside[1]), 0, rows, [])
    known = [(0, early)] + [(begin, sibling(x)) for (begin, _), x in zip(cuts, aside)]
    density = forward(units[-1:], 0, rows, known).reshape(own_count, width, aux)
    for p in range(PIECES):
        share = after(totals[p], known, *(arrived if p else []))
        sent = back(me_ref, packet, slots, own_count, share, groups)
        arrived = [to_group(block, k + 1) for k, block in enumerate(sent)]
        density = finish(me_ref, packets, slots, totals[p], arrived, density, p * part_width)
    return density


def solution(mesh):
    in_specs = (P("grp", "blk", None), P("grp", None), P("grp"), P(), P("blk"))
    out_specs = P("grp", "blk", None)
    return jax.shard_map(body, mesh=mesh, in_specs=in_specs, out_specs=out_specs, check_vma=False)
```

```python
import functools

import jax
import jax.numpy as jnp
from jax import lax
from jax.experimental import pallas as pl
from jax.experimental.pallas import tpu as pltpu
from jax.sharding import PartitionSpec as P

PIECES = 2
CORES = 2
SCALE = 1
VMEM = 56 * 1024 * 1024
ANY = pl.BlockSpec(memory_space=pl.ANY)
SMEM = pl.BlockSpec(memory_space=pltpu.SMEM)
LOCAL = pl.BlockSpec(memory_space=pltpu.VMEM)
PARAMS = pltpu.CompilerParams(vmem_limit_bytes=VMEM)


def split(x):
    high = x.astype(jnp.bfloat16)
    return high, (x - high.astype(jnp.float32)).astype(jnp.bfloat16)


def dot(a, b, contract):
    return lax.dot_general(a, b, ((contract[:1], contract[1:]), ((), ())), preferred_element_type=jnp.float32)


def block_rows(total, most):
    rows = most
    while total % rows:
        rows //= 2
    return rows


def after(x, *others):
    return lax.optimization_barrier((x, others))[0]


def cost(flops, moved):
    return pl.CostEstimate(flops=flops // SCALE, bytes_accessed=moved // SCALE, transcendentals=0)


def split_kernel(x_ref, high_ref, low_ref):
    high_ref[...], low_ref[...] = split(x_ref[...])


def split_rows(x):
    rows, width = x.shape
    step = block_rows(rows, 256)
    spec = pl.BlockSpec((step, width), lambda i: (i, 0))
    half = jax.ShapeDtypeStruct(x.shape, jnp.bfloat16)
    return pl.pallas_call(
        split_kernel,
        grid=(rows // step,),
        in_specs=[spec],
        out_specs=[spec, spec],
        out_shape=[half, half],
        cost_estimate=cost(2 * rows * width, 8 * rows * width),
        compiler_params=PARAMS,
    )(x)


def asked_row(lists, me, slots, own_count):
    asked, row = False, 0
    for s in range(slots):
        entry = lists[s]
        hit = lax.div(entry, own_count) == me
        asked = jnp.logical_or(asked, hit)
        row = jnp.where(hit, entry - me * own_count, row)
    return asked, row


def slot_holder(lists, me, s, own_count):
    return lax.bitwise_xor(lax.div(lists[s], own_count), me)


def pick_kernel(groups, slots, own_count, first, me_ref, *refs):
    lists, x_ref, outs, sem = refs[:groups], refs[groups], refs[groups + 1:-1], refs[-1]
    rows = outs[0].shape[0]
    copies = []
    for k in range(1, groups):
        _, row = asked_row(lists[k], me_ref[0], slots, own_count)
        copies.append(pltpu.make_async_copy(x_ref.at[row, pl.ds(first, rows)], outs[k - 1], sem.at[k - 1]))
        copies[-1].start()
    for copy in copies:
        copy.wait()


def pick(me, lists, slots, integrals, first, rows):
    own_count, _, aux = integrals.shape
    groups = len(lists)
    return pl.pallas_call(
        functools.partial(pick_kernel, groups, slots, own_count, first),
        in_specs=[SMEM] * (groups + 1) + [ANY],
        out_specs=[LOCAL] * (groups - 1),
        out_shape=[jax.ShapeDtypeStruct((rows, aux), jnp.float32)] * (groups - 1),
        scratch_shapes=[pltpu.SemaphoreType.DMA((groups - 1,))],
        cost_estimate=cost(0, 8 * rows * aux * groups),
        compiler_params=PARAMS,
    )(me, *lists, integrals)


def choose_kernel(groups, slots, own_count, first, me_ref, lists, x_ref, *refs):
    got, out, sem = refs[:groups - 1], refs[groups - 1], refs[groups]
    rows = out.shape[0] // slots
    me = me_ref[0]
    for s in range(slots):
        k_of = slot_holder(lists, me, s, own_count)
        to = out.at[pl.ds(s * rows, rows)]
        row = jnp.clip(lists[s] - me * own_count, 0, own_count - 1)

        @pl.when(k_of == 0)
        def _():
            pltpu.make_async_copy(x_ref.at[row, pl.ds(first, rows)], to, sem.at[s]).start()

        for k in range(1, groups):
            @pl.when(k_of == k)
            def _():
                pltpu.make_async_copy(got[k - 1], to, sem.at[s]).start()

        @pl.when(k_of >= groups)
        def _():
            to[...] = jnp.zeros_like(to)

    for s in range(slots):
        @pl.when(slot_holder(lists, me, s, own_count) < groups)
        def _():
            pltpu.make_async_copy(got[0], out.at[pl.ds(s * rows, rows)], sem.at[s]).wait()


def choose(me, lists, slots, integrals, got, first):
    own_count, _, aux = integrals.shape
    rows = got[0].shape[0]
    groups = len(got) + 1
    return pl.pallas_call(
        functools.partial(choose_kernel, groups, slots, own_count, first),
        in_specs=[SMEM, SMEM] + [ANY] * groups,
        out_specs=LOCAL,
        out_shape=jax.ShapeDtypeStruct((slots * rows, aux), jnp.float32),
        scratch_shapes=[pltpu.SemaphoreType.DMA((slots,))],
        cost_estimate=cost(0, 8 * rows * aux * slots),
        compiler_params=PARAMS,
    )(me, lists, integrals, *got)


def back_kernel(groups, slots, own_count, me_ref, lists, share, *refs):
    outs, sem = refs[:-1], refs[-1]
    rows = outs[0].shape[0]
    copies = []
    for k in range(1, groups):
        slot = 0
        for s in range(slots):
            slot = jnp.where(slot_holder(lists, me_ref[0], s, own_count) == k, s, slot)
        start = pl.multiple_of(slot * rows, rows)
        copies.append(pltpu.make_async_copy(share.at[pl.ds(start, rows)], outs[k - 1], sem.at[k - 1]))
        copies[-1].start()
    for copy in copies:
        copy.wait()


def back(me, lists, slots, own_count, share, groups):
    rows, aux = share.shape[0] // slots, share.shape[1]
    return pl.pallas_call(
        functools.partial(back_kernel, groups, slots, own_count),
        in_specs=[SMEM, SMEM, ANY],
        out_specs=[LOCAL] * (groups - 1),
        out_shape=[jax.ShapeDtypeStruct((rows, aux), jnp.float32)] * (groups - 1),
        scratch_shapes=[pltpu.SemaphoreType.DMA((groups - 1,))],
        cost_estimate=cost(0, 8 * rows * aux * groups),
        compiler_params=PARAMS,
    )(me, lists, share)


def finish_kernel(groups, slots, own_count, first, me_ref, *refs):
    lists, share, arrived = refs[:groups], refs[groups], refs[groups + 1:2 * groups]
    _, density, held, added, sem_held, sem_added = refs[2 * groups:]
    rows = held.shape[1]
    me = me_ref[0]
    asked, places, heads = [], [], []
    for k in range(groups):
        is_asked, row = asked_row(lists[k], me, slots, own_count)
        head = k
        for j in range(k - 1, -1, -1):
            head = jnp.where(jnp.logical_and(asked[j], places[j] == row), j, head)
        asked.append(is_asked)
        places.append(row)
        heads.append(head)
    slot = 0
    for s in range(slots):
        slot = jnp.where(slot_holder(lists[0], me, s, own_count) == 0, s, slot)
    start = pl.multiple_of(slot * rows, rows)
    leads = [jnp.logical_and(asked[k], heads[k] == k) for k in range(groups)]
    source = [share.at[pl.ds(start, rows)]] + list(arrived)
    spots = [density.at[places[k], pl.ds(first, rows)] for k in range(groups)]
    reads = [pltpu.make_async_copy(spots[k], held.at[k], sem_held.at[k]) for k in range(groups)]
    terms = [pltpu.make_async_copy(source[k], added.at[k], sem_added.at[k]) for k in range(groups)]
    writes = [pltpu.make_async_copy(held.at[k], spots[k], sem_held.at[k]) for k in range(groups)]
    for k in range(groups):
        pl.when(leads[k])(reads[k].start)
        pl.when(asked[k])(terms[k].start)
    for k in range(groups):
        pl.when(leads[k])(reads[k].wait)
    for k in range(groups):
        @pl.when(asked[k])
        def _():
            terms[k].wait()
            held[heads[k]] = held[heads[k]] + added[k]
    for k in range(groups):
        pl.when(leads[k])(writes[k].start)
    for k in range(groups):
        pl.when(leads[k])(writes[k].wait)


def finish(me, lists, slots, share, arrived, density, first):
    own_count, _, aux = density.shape
    groups = len(lists)
    rows = share.shape[0] // slots
    return pl.pallas_call(
        functools.partial(finish_kernel, groups, slots, own_count, first),
        in_specs=[SMEM] * (groups + 1) + [ANY] * (groups + 1),
        out_specs=ANY,
        out_shape=jax.ShapeDtypeStruct(density.shape, jnp.float32),
        input_output_aliases={2 * groups + 1: 0},
        scratch_shapes=[
            pltpu.VMEM((groups, rows, aux), jnp.float32),
            pltpu.VMEM((groups, rows, aux), jnp.float32),
            pltpu.SemaphoreType.DMA((groups,)),
            pltpu.SemaphoreType.DMA((groups,)),
        ],
        cost_estimate=cost(0, 12 * rows * aux * groups),
        compiler_params=PARAMS,
    )(me, *lists, share, *arrived, density)


def unit_kernel(steps, own_high, own_low, sib_high, sib_low, row_ref, col_ref, *refs):
    parts = refs[:PIECES]
    t_high, t_low, r_high, r_low = refs[PIECES:PIECES + 4]
    grads = refs[PIECES + 4:2 * PIECES + 4]
    step = pl.program_id(0)
    width = parts[0].shape[0]

    @pl.when(step == 0)
    def _():
        for p in range(PIECES):
            part = slice(p * width, (p + 1) * width)
            r_high[part], r_low[part] = split(parts[p][...])
            grads[p][...] = jnp.zeros_like(grads[p])

    def work(a_high, a_low):
        high, low = r_high[...], r_low[...]
        pair = dot(high, a_high[...], (1, 1)) + dot(low, a_high[...], (1, 1)) + dot(high, a_low[...], (1, 1))
        up, down = split(pair / (row_ref[...] + col_ref[...]))
        t_high[...] = up
        t_low[...] = down
        term = dot(up, a_high[...], (1, 0)) + dot(down, a_high[...], (1, 0)) + dot(up, a_low[...], (1, 0))
        for p in range(PIECES):
            grads[p][...] += term[p * width:(p + 1) * width]

    @pl.when(step < steps)
    def _():
        work(own_high, own_low)

    @pl.when(step >= steps)
    def _():
        work(sib_high, sib_low)


def unit(halves, row_energy, col_energy, parts):
    (own_high, own_low), (sib_high, sib_low) = halves
    rows, aux = own_high.shape
    step = block_rows(rows, 512)
    steps = rows // step
    part_rows = parts[0].shape[0]
    cols = part_rows * PIECES
    own = pl.BlockSpec((step, aux), lambda i: (jnp.minimum(i, steps - 1), 0))
    sib = pl.BlockSpec((step, aux), lambda i: (jnp.maximum(i - steps, 0), 0))
    whole = lambda shape: pl.BlockSpec(shape, lambda i: (0, 0))
    bf16 = lambda *shape: jax.ShapeDtypeStruct(shape, jnp.bfloat16)
    t_spec = pl.BlockSpec((cols, step), lambda i: (0, i))
    outs = pl.pallas_call(
        functools.partial(unit_kernel, steps),
        grid=(2 * steps,),
        in_specs=[own, own, sib, sib, pl.BlockSpec((1, step), lambda i: (0, i)), whole((cols, 1))]
        + [whole((part_rows, aux))] * PIECES,
        out_specs=[t_spec, t_spec, whole((cols, aux)), whole((cols, aux))] + [whole((part_rows, aux))] * PIECES,
        out_shape=[bf16(cols, 2 * rows)] * 2 + [bf16(cols, aux)] * 2
        + [jax.ShapeDtypeStruct((part_rows, aux), jnp.float32)] * PIECES,
        cost_estimate=cost(24 * rows * aux * cols, 8 * rows * aux + 16 * cols * aux),
        compiler_params=PARAMS,
    )(own_high, own_low, sib_high, sib_low, row_energy, col_energy, *parts)
    return outs[:4], outs[4:]


def forward_kernel(count, spans, *refs):
    out = refs[-1]
    total = None
    for u in range(count):
        t_high, t_low, r_high, r_low = (ref[...] for ref in refs[4 * u:4 * u + 4])
        term = dot(t_high, r_high, (0, 0)) + dot(t_high, r_low, (0, 0)) + dot(t_low, r_high, (0, 0))
        total = term if total is None else total + term
    out[...] = total
    step = pl.program_id(0)
    for (begin, end), start in zip(spans, refs[4 * count:-1]):
        @pl.when(jnp.logical_and(step >= begin, step < end))
        def _():
            out[...] += start[...]


def forward(units, first, count, starts):
    cols, aux = units[0][2].shape
    step = block_rows(count, 256)
    steps = count // step
    spans = [(begin // step, (begin + rows.shape[0]) // step) for begin, rows in starts]
    t_spec = pl.BlockSpec((cols, step), lambda i: (0, i + first // step))
    r_spec = pl.BlockSpec((cols, aux), lambda i: (0, 0))
    out_spec = pl.BlockSpec((step, aux), lambda i: (i, 0))
    start_spec = lambda begin, end: pl.BlockSpec((step, aux), lambda i: (jnp.clip(i, begin, end - 1) - begin, 0))
    return pl.pallas_call(
        functools.partial(forward_kernel, len(units), spans),
        grid=(steps,),
        in_specs=[t_spec, t_spec, r_spec, r_spec] * len(units) + [start_spec(*span) for span in spans],
        out_specs=out_spec,
        out_shape=jax.ShapeDtypeStruct((count, aux), jnp.float32),
        cost_estimate=cost(6 * count * aux * cols * len(units), 8 * count * aux),
        compiler_params=PARAMS,
    )(*(x for one in units for x in one), *(rows for _, rows in starts))


def ring_order(chips):
    return [0] + list(range(1, chips, 2)) + [z for z in range(chips - 1, 0, -1) if z % 2 == 0]


def body(integrals, pair_lists, row_orbital, occ_energy, vir_energy):
    own_count, width, aux = integrals.shape
    slots = pair_lists.shape[1]
    groups = lax.axis_size("grp")
    me = lax.axis_index("grp")
    me_ref = me.astype(jnp.int32).reshape(1)
    chips = lax.axis_size("blk") // CORES
    order = ring_order(chips)
    ring = lambda s: [
        (order[i] * CORES + c, order[(i + s) % chips] * CORES + c) for i in range(chips) for c in range(CORES)
    ]
    swap = [(i, i ^ 1) for i in range(chips * CORES)]
    along = lambda x, s: lax.ppermute(x, "blk", ring(s))
    hop = lambda x: along(x, 1)
    sibling = lambda x: lax.ppermute(x, "blk", swap)
    to_group = lambda x, k: lax.ppermute(x, "grp", [(g, g ^ k) for g in range(groups)])

    packet = jnp.concatenate([pair_lists[0], row_orbital])
    packets = [packet] + [to_group(packet, k) for k in range(1, groups)]
    own_rows = integrals.reshape(own_count * width, aux)
    sib_rows = sibling(own_rows)

    part_width = width // PIECES
    blocks = [pick(me_ref, packets, slots, integrals, p * part_width, part_width) for p in range(PIECES)]

    own_half = split_rows(after(own_rows, *blocks[-1]))

    ids = lax.broadcasted_iota(jnp.int32, (groups, own_count, occ_energy.shape[0]), 2)
    orbitals = jnp.stack(packets)[:, slots:]
    row_energies = jnp.sum(jnp.where(orbitals[:, :, None] == ids, occ_energy, 0.0), axis=2)
    held_rows = lax.bitwise_xor(lax.broadcasted_iota(jnp.int32, (groups, own_count), 0), me) * own_count
    held_rows = held_rows + lax.broadcasted_iota(jnp.int32, (groups, own_count), 1)
    listed_here = pair_lists[0][:, None, None] == held_rows
    partner_energy = jnp.sum(jnp.where(listed_here, row_energies, 0.0), axis=(1, 2))
    sib_virtual = sibling(vir_energy)
    row_energy = row_energies[0][None, :, None] - jnp.stack([vir_energy, sib_virtual])[:, None, :]
    row_energy = row_energy.reshape(1, CORES * own_count * width)
    virtual = [vir_energy] + [along(vir_energy, s) for s in range(1, chips)]
    early_energies = [sib_virtual] + virtual[1:]
    virtual = jnp.stack(virtual)
    col_energy = partner_energy[None, None, :, None] - virtual.reshape(chips, PIECES, 1, part_width)
    col_energy = list(col_energy.reshape(chips, slots * width, 1))

    pieces = []
    for p in range(PIECES):
        sent = blocks[p]
        got = [to_group(block, k + 1) for k, block in enumerate(sent)]
        if p == 1:
            halves = (own_half, split_rows(after(sib_rows, pieces[0][0])))
        got = after(got, halves, row_energy, col_energy, pieces[-1][0]) if p else after(got, own_half, early_energies)
        part = choose(me_ref, packet, slots, integrals, got, p * part_width)
        pieces.append([part, hop(part)])
        if p == 1:
            pieces[0][1] = after(pieces[0][1], halves)
    parts = [piece[0] for piece in pieces]
    first = [piece[1] for piece in pieces]

    units = []
    grads = []
    for s in range(chips):
        if s == 1:
            parts = first
        elif s:
            parts = [hop(x) for x in parts]
        ready = list(parts)
        if s == 0:
            ready[1] = after(ready[1], first[0])
        if s == 1:
            ready = after(ready, *grads[0])
        if s == chips - 1:
            totals = [hop(after(grad, parts[0], *grads[-1])) for grad in grads[1]]
        one, grad = unit(halves, row_energy, col_energy[s], ready)
        units.append(one)
        grads.append(grad)
    rows = own_count * width
    step = block_rows(rows, 256)
    last = rows - step
    middle = 0
    last = rows // 2
    cuts = [(0, last), (last, rows)]
    aside = []
    for s in range(2, chips + 1):
        done = totals
        if s == 2:
            totals[0] = after(totals[0], *grads[-1])
        totals = [x + y for x, y in zip(totals, grads[s % chips])]
        if s == 2:
            aside.append(forward(after(units, *done), rows, last, []))
        if s == chips - 1:
            most = forward(after(units[:-1], done[0], aside[0]), rows + last, rows - last, [])
            ready = after(units, most, *done)
            aside.append(forward(ready[-1:], rows + last, rows - last, [(0, most)]))
        if s < chips:
            totals = [hop(x) for x in totals]

    early = forward(after(units[:-1], aside[1]), 0, rows, [])
    known = [(0, early)] + [(begin, sibling(x)) for (begin, _), x in zip(cuts, aside)]
    density = forward(units[-1:], 0, rows, known).reshape(own_count, width, aux)
    product = density
    for p in range(PIECES):
        share = after(totals[p], known, *([product] + arrived if p else []))
        sent = back(me_ref, packet, slots, own_count, share, groups)
        arrived = [to_group(block, k + 1) for k, block in enumerate(sent)]
        density = finish(me_ref, packets, slots, totals[p], arrived, density, p * part_width)
    return density


def solution(mesh):
    in_specs = (P("grp", "blk", None), P("grp", None), P("grp"), P(), P("blk"))
    out_specs = P("grp", "blk", None)
    return jax.shard_map(body, mesh=mesh, in_specs=in_specs, out_specs=out_specs, check_vma=False)
```

```python
import functools

import jax
import jax.numpy as jnp
from jax import lax
from jax.experimental import pallas as pl
from jax.experimental.pallas import tpu as pltpu
from jax.sharding import PartitionSpec as P

PIECES = 2
CORES = 2
SCALE = 1
VMEM = 56 * 1024 * 1024
ANY = pl.BlockSpec(memory_space=pl.ANY)
SMEM = pl.BlockSpec(memory_space=pltpu.SMEM)
LOCAL = pl.BlockSpec(memory_space=pltpu.VMEM)
PARAMS = pltpu.CompilerParams(vmem_limit_bytes=VMEM)


def split(x):
    high = x.astype(jnp.bfloat16)
    return high, (x - high.astype(jnp.float32)).astype(jnp.bfloat16)


def dot(a, b, contract):
    return lax.dot_general(a, b, ((contract[:1], contract[1:]), ((), ())), preferred_element_type=jnp.float32)


def block_rows(total, most):
    rows = most
    while total % rows:
        rows //= 2
    return rows


def after(x, *others):
    return lax.optimization_barrier((x, others))[0]


def cost(flops, moved):
    return pl.CostEstimate(flops=flops // SCALE, bytes_accessed=moved // SCALE, transcendentals=0)


def split_kernel(x_ref, high_ref, low_ref):
    high_ref[...], low_ref[...] = split(x_ref[...])


def split_rows(x):
    rows, width = x.shape
    step = block_rows(rows, 256)
    spec = pl.BlockSpec((step, width), lambda i: (i, 0))
    half = jax.ShapeDtypeStruct(x.shape, jnp.bfloat16)
    return pl.pallas_call(
        split_kernel,
        grid=(rows // step,),
        in_specs=[spec],
        out_specs=[spec, spec],
        out_shape=[half, half],
        cost_estimate=cost(2 * rows * width, 8 * rows * width),
        compiler_params=PARAMS,
    )(x)


def asked_row(lists, me, slots, own_count):
    asked, row = False, 0
    for s in range(slots):
        entry = lists[s]
        hit = lax.div(entry, own_count) == me
        asked = jnp.logical_or(asked, hit)
        row = jnp.where(hit, entry - me * own_count, row)
    return asked, row


def slot_holder(lists, me, s, own_count):
    return lax.bitwise_xor(lax.div(lists[s], own_count), me)


def pick_kernel(groups, slots, own_count, first, me_ref, *refs):
    lists, x_ref, outs, sem = refs[:groups], refs[groups], refs[groups + 1:-1], refs[-1]
    rows = outs[0].shape[0]
    copies = []
    for k in range(1, groups):
        _, row = asked_row(lists[k], me_ref[0], slots, own_count)
        copies.append(pltpu.make_async_copy(x_ref.at[row, pl.ds(first, rows)], outs[k - 1], sem.at[k - 1]))
        copies[-1].start()
    for copy in copies:
        copy.wait()


def pick(me, lists, slots, integrals, first, rows):
    own_count, _, aux = integrals.shape
    groups = len(lists)
    return pl.pallas_call(
        functools.partial(pick_kernel, groups, slots, own_count, first),
        in_specs=[SMEM] * (groups + 1) + [ANY],
        out_specs=[LOCAL] * (groups - 1),
        out_shape=[jax.ShapeDtypeStruct((rows, aux), jnp.float32)] * (groups - 1),
        scratch_shapes=[pltpu.SemaphoreType.DMA((groups - 1,))],
        cost_estimate=cost(0, 8 * rows * aux * groups),
        compiler_params=PARAMS,
    )(me, *lists, integrals)


def choose_kernel(groups, slots, own_count, first, me_ref, lists, x_ref, *refs):
    got, out, sem = refs[:groups - 1], refs[groups - 1], refs[groups]
    rows = out.shape[0] // slots
    me = me_ref[0]
    for s in range(slots):
        k_of = slot_holder(lists, me, s, own_count)
        to = out.at[pl.ds(s * rows, rows)]
        row = jnp.clip(lists[s] - me * own_count, 0, own_count - 1)

        @pl.when(k_of == 0)
        def _():
            pltpu.make_async_copy(x_ref.at[row, pl.ds(first, rows)], to, sem.at[s]).start()

        for k in range(1, groups):
            @pl.when(k_of == k)
            def _():
                pltpu.make_async_copy(got[k - 1], to, sem.at[s]).start()

        @pl.when(k_of >= groups)
        def _():
            to[...] = jnp.zeros_like(to)

    for s in range(slots):
        @pl.when(slot_holder(lists, me, s, own_count) < groups)
        def _():
            pltpu.make_async_copy(got[0], out.at[pl.ds(s * rows, rows)], sem.at[s]).wait()


def choose(me, lists, slots, integrals, got, first):
    own_count, _, aux = integrals.shape
    rows = got[0].shape[0]
    groups = len(got) + 1
    return pl.pallas_call(
        functools.partial(choose_kernel, groups, slots, own_count, first),
        in_specs=[SMEM, SMEM] + [ANY] * groups,
        out_specs=LOCAL,
        out_shape=jax.ShapeDtypeStruct((slots * rows, aux), jnp.float32),
        scratch_shapes=[pltpu.SemaphoreType.DMA((slots,))],
        cost_estimate=cost(0, 8 * rows * aux * slots),
        compiler_params=PARAMS,
    )(me, lists, integrals, *got)


def back_kernel(groups, slots, own_count, me_ref, lists, share, *refs):
    outs, sem = refs[:-1], refs[-1]
    rows = outs[0].shape[0]
    copies = []
    for k in range(1, groups):
        slot = 0
        for s in range(slots):
            slot = jnp.where(slot_holder(lists, me_ref[0], s, own_count) == k, s, slot)
        start = pl.multiple_of(slot * rows, rows)
        copies.append(pltpu.make_async_copy(share.at[pl.ds(start, rows)], outs[k - 1], sem.at[k - 1]))
        copies[-1].start()
    for copy in copies:
        copy.wait()


def back(me, lists, slots, own_count, share, groups):
    rows, aux = share.shape[0] // slots, share.shape[1]
    return pl.pallas_call(
        functools.partial(back_kernel, groups, slots, own_count),
        in_specs=[SMEM, SMEM, ANY],
        out_specs=[LOCAL] * (groups - 1),
        out_shape=[jax.ShapeDtypeStruct((rows, aux), jnp.float32)] * (groups - 1),
        scratch_shapes=[pltpu.SemaphoreType.DMA((groups - 1,))],
        cost_estimate=cost(0, 8 * rows * aux * groups),
        compiler_params=PARAMS,
    )(me, lists, share)


def finish_kernel(groups, slots, own_count, me_ref, *refs):
    lists, refs = refs[:groups], refs[groups:]
    shares, refs = refs[:PIECES], refs[PIECES:]
    arrived = refs[:PIECES * (groups - 1)]
    _, density, held, added, sem_held, sem_added = refs[PIECES * (groups - 1):]
    rows = held.shape[1]
    me = me_ref[0]
    asked, places, heads = [], [], []
    for k in range(groups):
        is_asked, row = asked_row(lists[k], me, slots, own_count)
        head = k
        for j in range(k - 1, -1, -1):
            head = jnp.where(jnp.logical_and(asked[j], places[j] == row), j, head)
        asked.append(is_asked)
        places.append(row)
        heads.append(head)
    slot = 0
    for s in range(slots):
        slot = jnp.where(slot_holder(lists[0], me, s, own_count) == 0, s, slot)
    start = pl.multiple_of(slot * rows, rows)
    leads = [jnp.logical_and(asked[k], heads[k] == k) for k in range(groups)]
    every = [(p, k) for p in range(PIECES) for k in range(groups)]
    reads, terms, writes = {}, {}, {}
    for n, (p, k) in enumerate(every):
        source = arrived[p * (groups - 1) + k - 1] if k else shares[p].at[pl.ds(start, rows)]
        spot = density.at[places[k], pl.ds(p * rows, rows)]
        reads[p, k] = pltpu.make_async_copy(spot, held.at[n], sem_held.at[n])
        writes[p, k] = pltpu.make_async_copy(held.at[n], spot, sem_held.at[n])
        terms[p, k] = pltpu.make_async_copy(source, added.at[n], sem_added.at[n])
    for p, k in every:
        pl.when(leads[k])(reads[p, k].start)
        pl.when(asked[k])(terms[p, k].start)
    for p, k in every:
        pl.when(leads[k])(reads[p, k].wait)
    for n, (p, k) in enumerate(every):
        @pl.when(asked[k])
        def _():
            terms[p, k].wait()
            held[p * groups + heads[k]] = held[p * groups + heads[k]] + added[n]
    for p, k in every:
        pl.when(leads[k])(writes[p, k].start)
    for p, k in every:
        pl.when(leads[k])(writes[p, k].wait)


def finish(me, lists, slots, shares, arrived, density):
    own_count, _, aux = density.shape
    groups = len(lists)
    rows = shares[0].shape[0] // slots
    blocks = [block for piece in arrived for block in piece]
    operands = [me, *lists, *shares, *blocks, density]
    return pl.pallas_call(
        functools.partial(finish_kernel, groups, slots, own_count),
        in_specs=[SMEM] * (groups + 1) + [ANY] * (PIECES + len(blocks) + 1),
        out_specs=ANY,
        out_shape=jax.ShapeDtypeStruct(density.shape, jnp.float32),
        input_output_aliases={len(operands) - 1: 0},
        scratch_shapes=[pltpu.VMEM((PIECES * groups, rows, aux), jnp.float32)] * 2
        + [pltpu.SemaphoreType.DMA((PIECES * groups,))] * 2,
        cost_estimate=cost(0, 12 * rows * aux * groups * PIECES),
        compiler_params=PARAMS,
    )(*operands)


def unit_kernel(steps, own_high, own_low, sib_high, sib_low, row_ref, col_ref, *refs):
    parts = refs[:PIECES]
    t_high, t_low, r_high, r_low = refs[PIECES:PIECES + 4]
    grads = refs[PIECES + 4:2 * PIECES + 4]
    step = pl.program_id(0)
    width = parts[0].shape[0]

    @pl.when(step == 0)
    def _():
        for p in range(PIECES):
            part = slice(p * width, (p + 1) * width)
            r_high[part], r_low[part] = split(parts[p][...])
            grads[p][...] = jnp.zeros_like(grads[p])

    def work(a_high, a_low):
        high, low = r_high[...], r_low[...]
        pair = dot(high, a_high[...], (1, 1)) + dot(low, a_high[...], (1, 1)) + dot(high, a_low[...], (1, 1))
        up, down = split(pair / (row_ref[...] + col_ref[...]))
        t_high[...] = up
        t_low[...] = down
        term = dot(up, a_high[...], (1, 0)) + dot(down, a_high[...], (1, 0)) + dot(up, a_low[...], (1, 0))
        for p in range(PIECES):
            grads[p][...] += term[p * width:(p + 1) * width]

    @pl.when(step < steps)
    def _():
        work(own_high, own_low)

    @pl.when(step >= steps)
    def _():
        work(sib_high, sib_low)


def unit(halves, row_energy, col_energy, parts):
    (own_high, own_low), (sib_high, sib_low) = halves
    rows, aux = own_high.shape
    step = block_rows(rows, 512)
    steps = rows // step
    part_rows = parts[0].shape[0]
    cols = part_rows * PIECES
    own = pl.BlockSpec((step, aux), lambda i: (jnp.minimum(i, steps - 1), 0))
    sib = pl.BlockSpec((step, aux), lambda i: (jnp.maximum(i - steps, 0), 0))
    whole = lambda shape: pl.BlockSpec(shape, lambda i: (0, 0))
    bf16 = lambda *shape: jax.ShapeDtypeStruct(shape, jnp.bfloat16)
    t_spec = pl.BlockSpec((cols, step), lambda i: (0, i))
    outs = pl.pallas_call(
        functools.partial(unit_kernel, steps),
        grid=(2 * steps,),
        in_specs=[own, own, sib, sib, pl.BlockSpec((1, step), lambda i: (0, i)), whole((cols, 1))]
        + [whole((part_rows, aux))] * PIECES,
        out_specs=[t_spec, t_spec, whole((cols, aux)), whole((cols, aux))] + [whole((part_rows, aux))] * PIECES,
        out_shape=[bf16(cols, 2 * rows)] * 2 + [bf16(cols, aux)] * 2
        + [jax.ShapeDtypeStruct((part_rows, aux), jnp.float32)] * PIECES,
        cost_estimate=cost(24 * rows * aux * cols, 8 * rows * aux + 16 * cols * aux),
        compiler_params=PARAMS,
    )(own_high, own_low, sib_high, sib_low, row_energy, col_energy, *parts)
    return outs[:4], outs[4:]


def forward_kernel(count, spans, *refs):
    out = refs[-1]
    total = None
    for u in range(count):
        t_high, t_low, r_high, r_low = (ref[...] for ref in refs[4 * u:4 * u + 4])
        term = dot(t_high, r_high, (0, 0)) + dot(t_high, r_low, (0, 0)) + dot(t_low, r_high, (0, 0))
        total = term if total is None else total + term
    out[...] = total
    step = pl.program_id(0)
    for (begin, end), start in zip(spans, refs[4 * count:-1]):
        @pl.when(jnp.logical_and(step >= begin, step < end))
        def _():
            out[...] += start[...]


def forward(units, first, count, starts):
    cols, aux = units[0][2].shape
    step = block_rows(count, 256)
    steps = count // step
    spans = [(begin // step, (begin + rows.shape[0]) // step) for begin, rows in starts]
    t_spec = pl.BlockSpec((cols, step), lambda i: (0, i + first // step))
    r_spec = pl.BlockSpec((cols, aux), lambda i: (0, 0))
    out_spec = pl.BlockSpec((step, aux), lambda i: (i, 0))
    start_spec = lambda begin, end: pl.BlockSpec((step, aux), lambda i: (jnp.clip(i, begin, end - 1) - begin, 0))
    return pl.pallas_call(
        functools.partial(forward_kernel, len(units), spans),
        grid=(steps,),
        in_specs=[t_spec, t_spec, r_spec, r_spec] * len(units) + [start_spec(*span) for span in spans],
        out_specs=out_spec,
        out_shape=jax.ShapeDtypeStruct((count, aux), jnp.float32),
        cost_estimate=cost(6 * count * aux * cols * len(units), 8 * count * aux),
        compiler_params=PARAMS,
    )(*(x for one in units for x in one), *(rows for _, rows in starts))


def ring_order(chips):
    return [0] + list(range(1, chips, 2)) + [z for z in range(chips - 1, 0, -1) if z % 2 == 0]


def body(integrals, pair_lists, row_orbital, occ_energy, vir_energy):
    own_count, width, aux = integrals.shape
    slots = pair_lists.shape[1]
    groups = lax.axis_size("grp")
    me = lax.axis_index("grp")
    me_ref = me.astype(jnp.int32).reshape(1)
    chips = lax.axis_size("blk") // CORES
    order = ring_order(chips)
    ring = lambda s: [
        (order[i] * CORES + c, order[(i + s) % chips] * CORES + c) for i in range(chips) for c in range(CORES)
    ]
    swap = [(i, i ^ 1) for i in range(chips * CORES)]
    along = lambda x, s: lax.ppermute(x, "blk", ring(s))
    hop = lambda x: along(x, 1)
    sibling = lambda x: lax.ppermute(x, "blk", swap)
    to_group = lambda x, k: lax.ppermute(x, "grp", [(g, g ^ k) for g in range(groups)])

    packet = jnp.concatenate([pair_lists[0], row_orbital])
    packets = [packet] + [to_group(packet, k) for k in range(1, groups)]
    own_rows = integrals.reshape(own_count * width, aux)
    sib_rows = sibling(own_rows)

    part_width = width // PIECES
    blocks = [pick(me_ref, packets, slots, integrals, p * part_width, part_width) for p in range(PIECES)]

    own_half = split_rows(after(own_rows, *blocks[-1]))

    ids = lax.broadcasted_iota(jnp.int32, (groups, own_count, occ_energy.shape[0]), 2)
    orbitals = jnp.stack(packets)[:, slots:]
    row_energies = jnp.sum(jnp.where(orbitals[:, :, None] == ids, occ_energy, 0.0), axis=2)
    held_rows = lax.bitwise_xor(lax.broadcasted_iota(jnp.int32, (groups, own_count), 0), me) * own_count
    held_rows = held_rows + lax.broadcasted_iota(jnp.int32, (groups, own_count), 1)
    listed_here = pair_lists[0][:, None, None] == held_rows
    partner_energy = jnp.sum(jnp.where(listed_here, row_energies, 0.0), axis=(1, 2))
    sib_virtual = sibling(vir_energy)
    row_energy = row_energies[0][None, :, None] - jnp.stack([vir_energy, sib_virtual])[:, None, :]
    row_energy = row_energy.reshape(1, CORES * own_count * width)
    virtual = [vir_energy] + [along(vir_energy, s) for s in range(1, chips)]
    early_energies = [sib_virtual] + virtual[1:]
    virtual = jnp.stack(virtual)
    col_energy = partner_energy[None, None, :, None] - virtual.reshape(chips, PIECES, 1, part_width)
    col_energy = list(col_energy.reshape(chips, slots * width, 1))

    pieces = []
    for p in range(PIECES):
        sent = blocks[p]
        got = [to_group(block, k + 1) for k, block in enumerate(sent)]
        if p == 1:
            halves = (own_half, split_rows(after(sib_rows, pieces[0][0])))
        got = after(got, halves, pieces[-1][0]) if p else after(got, own_half, early_energies)
        part = choose(me_ref, packet, slots, integrals, got, p * part_width)
        pieces.append([part, hop(part)])
        if p == 1:
            pieces[0][1] = after(pieces[0][1], halves)
    parts = [piece[0] for piece in pieces]
    first = [piece[1] for piece in pieces]

    units = []
    grads = []
    for s in range(chips):
        if s == 1:
            parts = first
        elif s:
            parts = [hop(x) for x in parts]
        ready = list(parts)
        if s == 0:
            ready[1] = after(ready[1], first[0])
        if s == 1:
            ready = after(ready, *grads[0])
        if s == chips - 1:
            totals = [hop(after(grad, parts[0], *grads[-1])) for grad in grads[1]]
        one, grad = unit(halves, row_energy, col_energy[s], ready)
        units.append(one)
        grads.append(grad)
    rows = own_count * width
    step = block_rows(rows, 256)
    last = rows - step
    middle = 0
    last = rows // 2
    cuts = [(0, last), (last, rows)]
    aside = []
    for s in range(2, chips + 1):
        done = totals
        if s == 2:
            totals[0] = after(totals[0], *grads[-1])
        totals = [x + y for x, y in zip(totals, grads[s % chips])]
        if s == 2:
            aside.append(forward(after(units, *done), rows, last, []))
        if s == chips - 1:
            most = forward(after(units[:-1], done[0], aside[0]), rows + last, rows - last, [])
            ready = after(units, most, *done)
            aside.append(forward(ready[-1:], rows + last, rows - last, [(0, most)]))
        if s < chips:
            totals = [hop(x) for x in totals]

    early = forward(after(units[:-1], aside[1]), 0, rows, [])
    known = [(0, early)] + [(begin, sibling(x)) for (begin, _), x in zip(cuts, aside)]
    density = forward(units[-1:], 0, rows, known).reshape(own_count, width, aux)
    arrived = []
    for p in range(PIECES):
        share = after(totals[p], known, *(arrived[-1] if p else []))
        sent = back(me_ref, packet, slots, own_count, share, groups)
        arrived.append([to_group(block, k + 1) for k, block in enumerate(sent)])
    return finish(me_ref, packets, slots, totals, arrived, density)


def solution(mesh):
    in_specs = (P("grp", "blk", None), P("grp", None), P("grp"), P(), P("blk"))
    out_specs = P("grp", "blk", None)
    return jax.shard_map(body, mesh=mesh, in_specs=in_specs, out_specs=out_specs, check_vma=False)
```

```python
import functools

import jax
import jax.numpy as jnp
from jax import lax
from jax.experimental import pallas as pl
from jax.experimental.pallas import tpu as pltpu
from jax.sharding import PartitionSpec as P

PIECES = 2
CORES = 2
SCALE = 1
VMEM = 56 * 1024 * 1024
ANY = pl.BlockSpec(memory_space=pl.ANY)
SMEM = pl.BlockSpec(memory_space=pltpu.SMEM)
LOCAL = pl.BlockSpec(memory_space=pltpu.VMEM)
PARAMS = pltpu.CompilerParams(vmem_limit_bytes=VMEM)


def split(x):
    high = x.astype(jnp.bfloat16)
    return high, (x - high.astype(jnp.float32)).astype(jnp.bfloat16)


def dot(a, b, contract):
    return lax.dot_general(a, b, ((contract[:1], contract[1:]), ((), ())), preferred_element_type=jnp.float32)


def block_rows(total, most):
    rows = most
    while total % rows:
        rows //= 2
    return rows


def after(x, *others):
    return lax.optimization_barrier((x, others))[0]


def cost(flops, moved):
    return pl.CostEstimate(flops=flops // SCALE, bytes_accessed=moved // SCALE, transcendentals=0)


def split_kernel(x_ref, high_ref, low_ref):
    high_ref[...], low_ref[...] = split(x_ref[...])


def split_rows(x):
    rows, width = x.shape
    step = block_rows(rows, 256)
    spec = pl.BlockSpec((step, width), lambda i: (i, 0))
    half = jax.ShapeDtypeStruct(x.shape, jnp.bfloat16)
    return pl.pallas_call(
        split_kernel,
        grid=(rows // step,),
        in_specs=[spec],
        out_specs=[spec, spec],
        out_shape=[half, half],
        cost_estimate=cost(2 * rows * width, 8 * rows * width),
        compiler_params=PARAMS,
    )(x)


def asked_row(lists, me, slots, own_count):
    asked, row = False, 0
    for s in range(slots):
        entry = lists[s]
        hit = lax.div(entry, own_count) == me
        asked = jnp.logical_or(asked, hit)
        row = jnp.where(hit, entry - me * own_count, row)
    return asked, row


def slot_holder(lists, me, s, own_count):
    return lax.bitwise_xor(lax.div(lists[s], own_count), me)


def pick_kernel(groups, slots, own_count, first, me_ref, *refs):
    lists, x_ref, outs, sem = refs[:groups], refs[groups], refs[groups + 1:-1], refs[-1]
    rows = outs[0].shape[0]
    copies = []
    for k in range(1, groups):
        _, row = asked_row(lists[k], me_ref[0], slots, own_count)
        copies.append(pltpu.make_async_copy(x_ref.at[row, pl.ds(first, rows)], outs[k - 1], sem.at[k - 1]))
        copies[-1].start()
    for copy in copies:
        copy.wait()


def pick(me, lists, slots, integrals, first, rows):
    own_count, _, aux = integrals.shape
    groups = len(lists)
    return pl.pallas_call(
        functools.partial(pick_kernel, groups, slots, own_count, first),
        in_specs=[SMEM] * (groups + 1) + [ANY],
        out_specs=[LOCAL] * (groups - 1),
        out_shape=[jax.ShapeDtypeStruct((rows, aux), jnp.float32)] * (groups - 1),
        scratch_shapes=[pltpu.SemaphoreType.DMA((groups - 1,))],
        cost_estimate=cost(0, 8 * rows * aux * groups),
        compiler_params=PARAMS,
    )(me, *lists, integrals)


def choose_kernel(groups, slots, own_count, first, me_ref, lists, x_ref, *refs):
    got, out, sem = refs[:groups - 1], refs[groups - 1], refs[groups]
    rows = out.shape[0] // slots
    me = me_ref[0]
    for s in range(slots):
        k_of = slot_holder(lists, me, s, own_count)
        to = out.at[pl.ds(s * rows, rows)]
        row = jnp.clip(lists[s] - me * own_count, 0, own_count - 1)

        @pl.when(k_of == 0)
        def _():
            pltpu.make_async_copy(x_ref.at[row, pl.ds(first, rows)], to, sem.at[s]).start()

        for k in range(1, groups):
            @pl.when(k_of == k)
            def _():
                pltpu.make_async_copy(got[k - 1], to, sem.at[s]).start()

        @pl.when(k_of >= groups)
        def _():
            to[...] = jnp.zeros_like(to)

    for s in range(slots):
        @pl.when(slot_holder(lists, me, s, own_count) < groups)
        def _():
            pltpu.make_async_copy(got[0], out.at[pl.ds(s * rows, rows)], sem.at[s]).wait()


def choose(me, lists, slots, integrals, got, first):
    own_count, _, aux = integrals.shape
    rows = got[0].shape[0]
    groups = len(got) + 1
    return pl.pallas_call(
        functools.partial(choose_kernel, groups, slots, own_count, first),
        in_specs=[SMEM, SMEM] + [ANY] * groups,
        out_specs=LOCAL,
        out_shape=jax.ShapeDtypeStruct((slots * rows, aux), jnp.float32),
        scratch_shapes=[pltpu.SemaphoreType.DMA((slots,))],
        cost_estimate=cost(0, 8 * rows * aux * slots),
        compiler_params=PARAMS,
    )(me, lists, integrals, *got)


def back_kernel(groups, slots, own_count, me_ref, lists, share, *refs):
    outs, sem = refs[:-1], refs[-1]
    rows = outs[0].shape[0]
    copies = []
    for k in range(1, groups):
        slot = 0
        for s in range(slots):
            slot = jnp.where(slot_holder(lists, me_ref[0], s, own_count) == k, s, slot)
        start = pl.multiple_of(slot * rows, rows)
        copies.append(pltpu.make_async_copy(share.at[pl.ds(start, rows)], outs[k - 1], sem.at[k - 1]))
        copies[-1].start()
    for copy in copies:
        copy.wait()


def back(me, lists, slots, own_count, share, groups):
    rows, aux = share.shape[0] // slots, share.shape[1]
    return pl.pallas_call(
        functools.partial(back_kernel, groups, slots, own_count),
        in_specs=[SMEM, SMEM, ANY],
        out_specs=[LOCAL] * (groups - 1),
        out_shape=[jax.ShapeDtypeStruct((rows, aux), jnp.float32)] * (groups - 1),
        scratch_shapes=[pltpu.SemaphoreType.DMA((groups - 1,))],
        cost_estimate=cost(0, 8 * rows * aux * groups),
        compiler_params=PARAMS,
    )(me, lists, share)


def finish_kernel(groups, slots, own_count, me_ref, *refs):
    lists, refs = refs[:groups], refs[groups:]
    shares, refs = refs[:PIECES], refs[PIECES:]
    arrived = refs[:PIECES * (groups - 1)]
    _, density, held, added, sem_held, sem_added = refs[PIECES * (groups - 1):]
    rows = held.shape[1]
    me = me_ref[0]
    asked, places, heads = [], [], []
    for k in range(groups):
        is_asked, row = asked_row(lists[k], me, slots, own_count)
        head = k
        for j in range(k - 1, -1, -1):
            head = jnp.where(jnp.logical_and(asked[j], places[j] == row), j, head)
        asked.append(is_asked)
        places.append(row)
        heads.append(head)
    slot = 0
    for s in range(slots):
        slot = jnp.where(slot_holder(lists[0], me, s, own_count) == 0, s, slot)
    start = pl.multiple_of(slot * rows, rows)
    leads = [jnp.logical_and(asked[k], heads[k] == k) for k in range(groups)]
    every = [(p, k) for p in range(PIECES) for k in range(groups)]
    reads, terms, writes = {}, {}, {}
    for n, (p, k) in enumerate(every):
        source = arrived[p * (groups - 1) + k - 1] if k else shares[p].at[pl.ds(start, rows)]
        spot = density.at[places[k], pl.ds(p * rows, rows)]
        reads[p, k] = pltpu.make_async_copy(spot, held.at[n], sem_held.at[n])
        writes[p, k] = pltpu.make_async_copy(held.at[n], spot, sem_held.at[n])
        terms[p, k] = pltpu.make_async_copy(source, added.at[n], sem_added.at[n])
    for p, k in every:
        pl.when(leads[k])(reads[p, k].start)
        pl.when(asked[k])(terms[p, k].start)
    for p, k in every:
        pl.when(leads[k])(reads[p, k].wait)
    for n, (p, k) in enumerate(every):
        @pl.when(asked[k])
        def _():
            terms[p, k].wait()
            held[p * groups + heads[k]] = held[p * groups + heads[k]] + added[n]
    for p, k in every:
        pl.when(leads[k])(writes[p, k].start)
    for p, k in every:
        pl.when(leads[k])(writes[p, k].wait)


def finish(me, lists, slots, shares, arrived, density):
    own_count, _, aux = density.shape
    groups = len(lists)
    rows = shares[0].shape[0] // slots
    blocks = [block for piece in arrived for block in piece]
    operands = [me, *lists, *shares, *blocks, density]
    return pl.pallas_call(
        functools.partial(finish_kernel, groups, slots, own_count),
        in_specs=[SMEM] * (groups + 1) + [ANY] * (PIECES + len(blocks) + 1),
        out_specs=ANY,
        out_shape=jax.ShapeDtypeStruct(density.shape, jnp.float32),
        input_output_aliases={len(operands) - 1: 0},
        scratch_shapes=[pltpu.VMEM((PIECES * groups, rows, aux), jnp.float32)] * 2
        + [pltpu.SemaphoreType.DMA((PIECES * groups,))] * 2,
        cost_estimate=cost(0, 12 * rows * aux * groups * PIECES),
        compiler_params=PARAMS,
    )(*operands)


def unit_kernel(steps, own_high, own_low, sib_high, sib_low, row_ref, col_ref, *refs):
    parts = refs[:PIECES]
    t_high, t_low, r_high, r_low = refs[PIECES:PIECES + 4]
    grads = refs[PIECES + 4:2 * PIECES + 4]
    step = pl.program_id(0)
    width = parts[0].shape[0]

    @pl.when(step == 0)
    def _():
        for p in range(PIECES):
            part = slice(p * width, (p + 1) * width)
            r_high[part], r_low[part] = split(parts[p][...])
            grads[p][...] = jnp.zeros_like(grads[p])

    def work(a_high, a_low):
        high, low = r_high[...], r_low[...]
        pair = dot(high, a_high[...], (1, 1)) + dot(low, a_high[...], (1, 1)) + dot(high, a_low[...], (1, 1))
        up, down = split(pair / (row_ref[...] + col_ref[...]))
        t_high[...] = up
        t_low[...] = down
        term = dot(up, a_high[...], (1, 0)) + dot(down, a_high[...], (1, 0)) + dot(up, a_low[...], (1, 0))
        for p in range(PIECES):
            grads[p][...] += term[p * width:(p + 1) * width]

    @pl.when(step < steps)
    def _():
        work(own_high, own_low)

    @pl.when(step >= steps)
    def _():
        work(sib_high, sib_low)


def unit(halves, row_energy, col_energy, parts):
    (own_high, own_low), (sib_high, sib_low) = halves
    rows, aux = own_high.shape
    step = block_rows(rows, 512)
    steps = rows // step
    part_rows = parts[0].shape[0]
    cols = part_rows * PIECES
    own = pl.BlockSpec((step, aux), lambda i: (jnp.minimum(i, steps - 1), 0))
    sib = pl.BlockSpec((step, aux), lambda i: (jnp.maximum(i - steps, 0), 0))
    whole = lambda shape: pl.BlockSpec(shape, lambda i: (0, 0))
    bf16 = lambda *shape: jax.ShapeDtypeStruct(shape, jnp.bfloat16)
    t_spec = pl.BlockSpec((cols, step), lambda i: (0, i))
    outs = pl.pallas_call(
        functools.partial(unit_kernel, steps),
        grid=(2 * steps,),
        in_specs=[own, own, sib, sib, pl.BlockSpec((1, step), lambda i: (0, i)), whole((cols, 1))]
        + [whole((part_rows, aux))] * PIECES,
        out_specs=[t_spec, t_spec, whole((cols, aux)), whole((cols, aux))] + [whole((part_rows, aux))] * PIECES,
        out_shape=[bf16(cols, 2 * rows)] * 2 + [bf16(cols, aux)] * 2
        + [jax.ShapeDtypeStruct((part_rows, aux), jnp.float32)] * PIECES,
        cost_estimate=cost(24 * rows * aux * cols, 8 * rows * aux + 16 * cols * aux),
        compiler_params=PARAMS,
    )(own_high, own_low, sib_high, sib_low, row_energy, col_energy, *parts)
    return outs[:4], outs[4:]


def forward_kernel(count, spans, *refs):
    out = refs[-1]
    total = None
    for u in range(count):
        t_high, t_low, r_high, r_low = (ref[...] for ref in refs[4 * u:4 * u + 4])
        term = dot(t_high, r_high, (0, 0)) + dot(t_high, r_low, (0, 0)) + dot(t_low, r_high, (0, 0))
        total = term if total is None else total + term
    out[...] = total
    step = pl.program_id(0)
    for (begin, end), start in zip(spans, refs[4 * count:-1]):
        @pl.when(jnp.logical_and(step >= begin, step < end))
        def _():
            out[...] += start[...]


def forward(units, first, count, starts):
    cols, aux = units[0][2].shape
    step = block_rows(count, 256)
    steps = count // step
    spans = [(begin // step, (begin + rows.shape[0]) // step) for begin, rows in starts]
    t_spec = pl.BlockSpec((cols, step), lambda i: (0, i + first // step))
    r_spec = pl.BlockSpec((cols, aux), lambda i: (0, 0))
    out_spec = pl.BlockSpec((step, aux), lambda i: (i, 0))
    start_spec = lambda begin, end: pl.BlockSpec((step, aux), lambda i: (jnp.clip(i, begin, end - 1) - begin, 0))
    return pl.pallas_call(
        functools.partial(forward_kernel, len(units), spans),
        grid=(steps,),
        in_specs=[t_spec, t_spec, r_spec, r_spec] * len(units) + [start_spec(*span) for span in spans],
        out_specs=out_spec,
        out_shape=jax.ShapeDtypeStruct((count, aux), jnp.float32),
        cost_estimate=cost(6 * count * aux * cols * len(units), 8 * count * aux),
        compiler_params=PARAMS,
    )(*(x for one in units for x in one), *(rows for _, rows in starts))


def ring_order(chips):
    return [0] + list(range(1, chips, 2)) + [z for z in range(chips - 1, 0, -1) if z % 2 == 0]


def body(integrals, pair_lists, row_orbital, occ_energy, vir_energy):
    own_count, width, aux = integrals.shape
    slots = pair_lists.shape[1]
    groups = lax.axis_size("grp")
    me = lax.axis_index("grp")
    me_ref = me.astype(jnp.int32).reshape(1)
    chips = lax.axis_size("blk") // CORES
    order = ring_order(chips)
    ring = lambda s: [
        (order[i] * CORES + c, order[(i + s) % chips] * CORES + c) for i in range(chips) for c in range(CORES)
    ]
    swap = [(i, i ^ 1) for i in range(chips * CORES)]
    along = lambda x, s: lax.ppermute(x, "blk", ring(s))
    hop = lambda x: along(x, 1)
    sibling = lambda x: lax.ppermute(x, "blk", swap)
    to_group = lambda x, k: lax.ppermute(x, "grp", [(g, g ^ k) for g in range(groups)])

    packet = jnp.concatenate([pair_lists[0], row_orbital])
    packets = [packet] + [to_group(packet, k) for k in range(1, groups)]
    own_rows = integrals.reshape(own_count * width, aux)
    sib_rows = sibling(own_rows)

    part_width = width // PIECES
    blocks = [pick(me_ref, packets, slots, integrals, p * part_width, part_width) for p in range(PIECES)]

    own_half = split_rows(after(own_rows, *blocks[-1]))

    ids = lax.broadcasted_iota(jnp.int32, (groups, own_count, occ_energy.shape[0]), 2)
    orbitals = jnp.stack(packets)[:, slots:]
    row_energies = jnp.sum(jnp.where(orbitals[:, :, None] == ids, occ_energy, 0.0), axis=2)
    held_rows = lax.bitwise_xor(lax.broadcasted_iota(jnp.int32, (groups, own_count), 0), me) * own_count
    held_rows = held_rows + lax.broadcasted_iota(jnp.int32, (groups, own_count), 1)
    listed_here = pair_lists[0][:, None, None] == held_rows
    partner_energy = jnp.sum(jnp.where(listed_here, row_energies, 0.0), axis=(1, 2))
    sib_virtual = sibling(vir_energy)
    row_energy = row_energies[0][None, :, None] - jnp.stack([vir_energy, sib_virtual])[:, None, :]
    row_energy = row_energy.reshape(1, CORES * own_count * width)
    virtual = [vir_energy] + [along(vir_energy, s) for s in range(1, chips)]
    early_energies = [sib_virtual] + virtual[1:]
    virtual = jnp.stack(virtual)
    col_energy = partner_energy[None, None, :, None] - virtual.reshape(chips, PIECES, 1, part_width)
    col_energy = list(col_energy.reshape(chips, slots * width, 1))

    pieces = []
    for p in range(PIECES):
        sent = blocks[p]
        got = [to_group(block, k + 1) for k, block in enumerate(sent)]
        if p == 1:
            halves = (own_half, split_rows(after(sib_rows, pieces[0][0])))
        got = after(got, halves, pieces[-1][0]) if p else after(got, own_half, early_energies)
        part = choose(me_ref, packet, slots, integrals, got, p * part_width)
        pieces.append([part, hop(part)])
        if p == 1:
            pieces[0][1] = after(pieces[0][1], halves)
    parts = [piece[0] for piece in pieces]
    first = [piece[1] for piece in pieces]

    units = []
    grads = []
    for s in range(chips):
        if s == 1:
            parts = first
        elif s:
            parts = [hop(after(x, *grads[1]) if s == 3 and p == 0 else x) for p, x in enumerate(parts)]
        ready = list(parts)
        if s == 0:
            ready[1] = after(ready[1], first[0])
        if s == 1:
            ready = after(ready, *grads[0])
        if s == chips - 1:
            totals = [hop(after(grad, parts[0], *grads[-1])) for grad in grads[1]]
        one, grad = unit(halves, row_energy, col_energy[s], ready)
        units.append(one)
        grads.append(grad)
    rows = own_count * width
    step = block_rows(rows, 256)
    last = rows - step
    middle = 0
    last = rows // 2
    cuts = [(0, last), (last, rows)]
    aside = []
    for s in range(2, chips + 1):
        done = totals
        if s == 2:
            totals[0] = after(totals[0], *grads[-1])
        totals = [x + y for x, y in zip(totals, grads[s % chips])]
        if s == 2:
            aside.append(forward(after(units, *done), rows, last, []))
        if s == chips - 1:
            most = forward(after(units[:-1], done[0], aside[0]), rows + last, rows - last, [])
            ready = after(units, most, *done)
            aside.append(forward(ready[-1:], rows + last, rows - last, [(0, most)]))
        if s < chips:
            totals = [hop(x) for x in totals]

    early = forward(after(units[:-1], aside[1]), 0, rows, [])
    known = [(0, early)] + [(begin, sibling(x)) for (begin, _), x in zip(cuts, aside)]
    density = forward(units[-1:], 0, rows, known).reshape(own_count, width, aux)
    arrived = []
    for p in range(PIECES):
        share = after(totals[p], known, *(arrived[-1] if p else []))
        sent = back(me_ref, packet, slots, own_count, share, groups)
        arrived.append([to_group(block, k + 1) for k, block in enumerate(sent)])
    return finish(me_ref, packets, slots, totals, arrived, density)


def solution(mesh):
    in_specs = (P("grp", "blk", None), P("grp", None), P("grp"), P(), P("blk"))
    out_specs = P("grp", "blk", None)
    return jax.shard_map(body, mesh=mesh, in_specs=in_specs, out_specs=out_specs, check_vma=False)
```

```python
import functools
import math

import jax
import jax.numpy as jnp
from jax import lax
from jax.experimental import pallas as pl
from jax.experimental.pallas import tpu as pltpu
from jax.sharding import PartitionSpec as P

PIECES = 2
CORES = 2
SCALE = 1
VMEM = 56 * 1024 * 1024
ANY = pl.BlockSpec(memory_space=pl.ANY)
SMEM = pl.BlockSpec(memory_space=pltpu.SMEM)
LOCAL = pl.BlockSpec(memory_space=pltpu.VMEM)
PARAMS = pltpu.CompilerParams(vmem_limit_bytes=VMEM)


def split(x):
    high = x.astype(jnp.bfloat16)
    return high, (x - high.astype(jnp.float32)).astype(jnp.bfloat16)


def dot(a, b, contract):
    return lax.dot_general(a, b, ((contract[:1], contract[1:]), ((), ())), preferred_element_type=jnp.float32)


def block_rows(total, most):
    rows = most
    while total % rows:
        rows //= 2
    return rows


def after(x, *others):
    return lax.optimization_barrier((x, others))[0]


def cost(flops, moved):
    return pl.CostEstimate(flops=flops // SCALE, bytes_accessed=moved // SCALE, transcendentals=0)


def split_kernel(x_ref, high_ref, low_ref):
    high_ref[...], low_ref[...] = split(x_ref[...])


def split_rows(x):
    rows, width = x.shape
    step = block_rows(rows, 256)
    spec = pl.BlockSpec((step, width), lambda i: (i, 0))
    half = jax.ShapeDtypeStruct(x.shape, jnp.bfloat16)
    return pl.pallas_call(
        split_kernel,
        grid=(rows // step,),
        in_specs=[spec],
        out_specs=[spec, spec],
        out_shape=[half, half],
        cost_estimate=cost(2 * rows * width, 8 * rows * width),
        compiler_params=PARAMS,
    )(x)


def asked_row(lists, me, slots, own_count):
    asked, row = False, 0
    for s in range(slots):
        entry = lists[s]
        hit = lax.div(entry, own_count) == me
        asked = jnp.logical_or(asked, hit)
        row = jnp.where(hit, entry - me * own_count, row)
    return asked, row


def slot_holder(lists, me, s, own_count):
    return lax.bitwise_xor(lax.div(lists[s], own_count), me)


def pick_kernel(groups, slots, own_count, first, me_ref, *refs):
    lists, x_ref, outs, sem = refs[:groups], refs[groups], refs[groups + 1:-1], refs[-1]
    rows = outs[0].shape[0]
    copies = []
    for k in range(1, groups):
        _, row = asked_row(lists[k], me_ref[0], slots, own_count)
        copies.append(pltpu.make_async_copy(x_ref.at[row, pl.ds(first, rows)], outs[k - 1], sem.at[k - 1]))
        copies[-1].start()
    for copy in copies:
        copy.wait()


def pick(me, lists, slots, integrals, first, rows):
    own_count, _, aux = integrals.shape
    groups = len(lists)
    return pl.pallas_call(
        functools.partial(pick_kernel, groups, slots, own_count, first),
        in_specs=[SMEM] * (groups + 1) + [ANY],
        out_specs=[LOCAL] * (groups - 1),
        out_shape=[jax.ShapeDtypeStruct((rows, aux), jnp.float32)] * (groups - 1),
        scratch_shapes=[pltpu.SemaphoreType.DMA((groups - 1,))],
        cost_estimate=cost(0, 8 * rows * aux * groups),
        compiler_params=PARAMS,
    )(me, *lists, integrals)


def choose_kernel(groups, slots, own_count, first, me_ref, lists, x_ref, *refs):
    got, out, sem = refs[:groups - 1], refs[groups - 1], refs[groups]
    rows = out.shape[0] // slots
    me = me_ref[0]
    for s in range(slots):
        k_of = slot_holder(lists, me, s, own_count)
        to = out.at[pl.ds(s * rows, rows)]
        row = jnp.clip(lists[s] - me * own_count, 0, own_count - 1)

        @pl.when(k_of == 0)
        def _():
            pltpu.make_async_copy(x_ref.at[row, pl.ds(first, rows)], to, sem.at[s]).start()

        for k in range(1, groups):
            @pl.when(k_of == k)
            def _():
                pltpu.make_async_copy(got[k - 1], to, sem.at[s]).start()

        @pl.when(k_of >= groups)
        def _():
            to[...] = jnp.zeros_like(to)

    for s in range(slots):
        @pl.when(slot_holder(lists, me, s, own_count) < groups)
        def _():
            pltpu.make_async_copy(got[0], out.at[pl.ds(s * rows, rows)], sem.at[s]).wait()


def choose(me, lists, slots, integrals, got, first):
    own_count, _, aux = integrals.shape
    rows = got[0].shape[0]
    groups = len(got) + 1
    return pl.pallas_call(
        functools.partial(choose_kernel, groups, slots, own_count, first),
        in_specs=[SMEM, SMEM] + [ANY] * groups,
        out_specs=LOCAL,
        out_shape=jax.ShapeDtypeStruct((slots * rows, aux), jnp.float32),
        scratch_shapes=[pltpu.SemaphoreType.DMA((slots,))],
        cost_estimate=cost(0, 8 * rows * aux * slots),
        compiler_params=PARAMS,
    )(me, lists, integrals, *got)


def back_kernel(groups, slots, own_count, me_ref, lists, share, *refs):
    outs, sem = refs[:-1], refs[-1]
    rows = outs[0].shape[0]
    copies = []
    for k in range(1, groups):
        slot = 0
        for s in range(slots):
            slot = jnp.where(slot_holder(lists, me_ref[0], s, own_count) == k, s, slot)
        start = pl.multiple_of(slot * rows, rows)
        copies.append(pltpu.make_async_copy(share.at[pl.ds(start, rows)], outs[k - 1], sem.at[k - 1]))
        copies[-1].start()
    for copy in copies:
        copy.wait()


def back(me, lists, slots, own_count, share, groups):
    rows, aux = share.shape[0] // slots, share.shape[1]
    return pl.pallas_call(
        functools.partial(back_kernel, groups, slots, own_count),
        in_specs=[SMEM, SMEM, ANY],
        out_specs=[LOCAL] * (groups - 1),
        out_shape=[jax.ShapeDtypeStruct((rows, aux), jnp.float32)] * (groups - 1),
        scratch_shapes=[pltpu.SemaphoreType.DMA((groups - 1,))],
        cost_estimate=cost(0, 8 * rows * aux * groups),
        compiler_params=PARAMS,
    )(me, lists, share)


def finish_kernel(groups, slots, own_count, me_ref, *refs):
    lists, refs = refs[:groups], refs[groups:]
    shares, refs = refs[:PIECES], refs[PIECES:]
    arrived = refs[:PIECES * (groups - 1)]
    _, density, held, added, sem_held, sem_added = refs[PIECES * (groups - 1):]
    rows = held.shape[1]
    me = me_ref[0]
    asked, places, heads = [], [], []
    for k in range(groups):
        is_asked, row = asked_row(lists[k], me, slots, own_count)
        head = k
        for j in range(k - 1, -1, -1):
            head = jnp.where(jnp.logical_and(asked[j], places[j] == row), j, head)
        asked.append(is_asked)
        places.append(row)
        heads.append(head)
    slot = 0
    for s in range(slots):
        slot = jnp.where(slot_holder(lists[0], me, s, own_count) == 0, s, slot)
    start = pl.multiple_of(slot * rows, rows)
    leads = [jnp.logical_and(asked[k], heads[k] == k) for k in range(groups)]
    every = [(p, k) for p in range(PIECES) for k in range(groups)]
    reads, terms, writes = {}, {}, {}
    for n, (p, k) in enumerate(every):
        source = arrived[p * (groups - 1) + k - 1] if k else shares[p].at[pl.ds(start, rows)]
        spot = density.at[places[k], pl.ds(p * rows, rows)]
        reads[p, k] = pltpu.make_async_copy(spot, held.at[n], sem_held.at[n])
        writes[p, k] = pltpu.make_async_copy(held.at[n], spot, sem_held.at[n])
        terms[p, k] = pltpu.make_async_copy(source, added.at[n], sem_added.at[n])
    for p, k in every:
        pl.when(leads[k])(reads[p, k].start)
        pl.when(asked[k])(terms[p, k].start)
    for p, k in every:
        pl.when(leads[k])(reads[p, k].wait)
    for n, (p, k) in enumerate(every):
        @pl.when(asked[k])
        def _():
            terms[p, k].wait()
            held[p * groups + heads[k]] = held[p * groups + heads[k]] + added[n]
    for p, k in every:
        pl.when(leads[k])(writes[p, k].start)
    for p, k in every:
        pl.when(leads[k])(writes[p, k].wait)


def finish(me, lists, slots, shares, arrived, density):
    own_count, _, aux = density.shape
    groups = len(lists)
    rows = shares[0].shape[0] // slots
    blocks = [block for piece in arrived for block in piece]
    operands = [me, *lists, *shares, *blocks, density]
    return pl.pallas_call(
        functools.partial(finish_kernel, groups, slots, own_count),
        in_specs=[SMEM] * (groups + 1) + [ANY] * (PIECES + len(blocks) + 1),
        out_specs=ANY,
        out_shape=jax.ShapeDtypeStruct(density.shape, jnp.float32),
        input_output_aliases={len(operands) - 1: 0},
        scratch_shapes=[pltpu.VMEM((PIECES * groups, rows, aux), jnp.float32)] * 2
        + [pltpu.SemaphoreType.DMA((PIECES * groups,))] * 2,
        cost_estimate=cost(0, 12 * rows * aux * groups * PIECES),
        compiler_params=PARAMS,
    )(*operands)


def unit_kernel(steps, own_high, own_low, sib_high, sib_low, row_ref, col_ref, *refs):
    parts = refs[:PIECES]
    t_high, t_low, r_high, r_low = refs[PIECES:PIECES + 4]
    grads = refs[PIECES + 4:2 * PIECES + 4]
    step = pl.program_id(0)
    width = parts[0].shape[0]

    @pl.when(step == 0)
    def _():
        for p in range(PIECES):
            part = slice(p * width, (p + 1) * width)
            r_high[part], r_low[part] = split(parts[p][...])
            grads[p][...] = jnp.zeros_like(grads[p])

    def work(a_high, a_low):
        high, low = r_high[...], r_low[...]
        pair = dot(high, a_high[...], (1, 1)) + dot(low, a_high[...], (1, 1)) + dot(high, a_low[...], (1, 1))
        up, down = split(pair / (row_ref[...] + col_ref[...]))
        t_high[...] = up
        t_low[...] = down
        term = dot(up, a_high[...], (1, 0)) + dot(down, a_high[...], (1, 0)) + dot(up, a_low[...], (1, 0))
        for p in range(PIECES):
            grads[p][...] += term[p * width:(p + 1) * width]

    @pl.when(step < steps)
    def _():
        work(own_high, own_low)

    @pl.when(step >= steps)
    def _():
        work(sib_high, sib_low)


def unit(halves, row_energy, col_energy, parts):
    (own_high, own_low), (sib_high, sib_low) = halves
    rows, aux = own_high.shape
    step = block_rows(rows, 512)
    steps = rows // step
    part_rows = parts[0].shape[0]
    cols = part_rows * PIECES
    own = pl.BlockSpec((step, aux), lambda i: (jnp.minimum(i, steps - 1), 0))
    sib = pl.BlockSpec((step, aux), lambda i: (jnp.maximum(i - steps, 0), 0))
    whole = lambda shape: pl.BlockSpec(shape, lambda i: (0, 0))
    bf16 = lambda *shape: jax.ShapeDtypeStruct(shape, jnp.bfloat16)
    t_spec = pl.BlockSpec((cols, step), lambda i: (0, i))
    outs = pl.pallas_call(
        functools.partial(unit_kernel, steps),
        grid=(2 * steps,),
        in_specs=[own, own, sib, sib, pl.BlockSpec((1, step), lambda i: (0, i)), whole((cols, 1))]
        + [whole((part_rows, aux))] * PIECES,
        out_specs=[t_spec, t_spec, whole((cols, aux)), whole((cols, aux))] + [whole((part_rows, aux))] * PIECES,
        out_shape=[bf16(cols, 2 * rows)] * 2 + [bf16(cols, aux)] * 2
        + [jax.ShapeDtypeStruct((part_rows, aux), jnp.float32)] * PIECES,
        cost_estimate=cost(24 * rows * aux * cols, 8 * rows * aux + 16 * cols * aux),
        compiler_params=PARAMS,
    )(own_high, own_low, sib_high, sib_low, row_energy, col_energy, *parts)
    return outs[:4], outs[4:]


def forward_term(refs):
    t_high, t_low, r_high, r_low = (ref[...] for ref in refs)
    return dot(t_high, r_high, (0, 0)) + dot(t_high, r_low, (0, 0)) + dot(t_low, r_high, (0, 0))


def forward_kernel(count, spans, partial, *refs):
    out = refs[-1]
    total = None
    for u in range(count - partial):
        term = forward_term(refs[4 * u:4 * u + 4])
        total = term if total is None else total + term
    out[...] = total
    step = pl.program_id(0)
    if partial:
        @pl.when(step < pl.num_programs(0) - 1)
        def _():
            out[...] += forward_term(refs[4 * (count - 1):4 * count])
    for (begin, end), start in zip(spans, refs[4 * count:-1]):
        @pl.when(jnp.logical_and(step >= begin, step < end))
        def _():
            out[...] += start[...]


def forward(units, first, count, starts, partial=False):
    cols, aux = units[0][2].shape
    step = block_rows(math.gcd(count, *(begin for begin, _ in starts), *(rows.shape[0] for _, rows in starts)), 256)
    steps = count // step
    spans = [(begin // step, (begin + rows.shape[0]) // step) for begin, rows in starts]
    t_spec = pl.BlockSpec((cols, step), lambda i: (0, i + first // step))
    r_spec = pl.BlockSpec((cols, aux), lambda i: (0, 0))
    out_spec = pl.BlockSpec((step, aux), lambda i: (i, 0))
    start_spec = lambda begin, end: pl.BlockSpec((step, aux), lambda i: (jnp.clip(i, begin, end - 1) - begin, 0))
    return pl.pallas_call(
        functools.partial(forward_kernel, len(units), spans, partial),
        grid=(steps,),
        in_specs=[t_spec, t_spec, r_spec, r_spec] * len(units) + [start_spec(*span) for span in spans],
        out_specs=out_spec,
        out_shape=jax.ShapeDtypeStruct((count, aux), jnp.float32),
        cost_estimate=cost(6 * count * aux * cols * len(units), 8 * count * aux),
        compiler_params=PARAMS,
    )(*(x for one in units for x in one), *(rows for _, rows in starts))


def complete_kernel(t_high, t_low, r_high, r_low, known, out):
    out[...] = known[...] + forward_term((t_high, t_low, r_high, r_low))


def complete(unit_parts, first, known):
    cols, aux = unit_parts[2].shape
    count = known.shape[0]
    step = block_rows(count, 256)
    last = count // step - 1
    t_spec = pl.BlockSpec((cols, step), lambda i: (0, first // step + last))
    r_spec = pl.BlockSpec((cols, aux), lambda i: (0, 0))
    block = pl.BlockSpec((step, aux), lambda i: (last, 0))
    return pl.pallas_call(
        complete_kernel,
        grid=(1,),
        in_specs=[t_spec, t_spec, r_spec, r_spec, block],
        out_specs=block,
        out_shape=jax.ShapeDtypeStruct(known.shape, jnp.float32),
        input_output_aliases={4: 0},
        cost_estimate=cost(6 * count * aux * cols, 8 * count * aux),
        compiler_params=PARAMS,
    )(*unit_parts, known)


def ring_order(chips):
    return [0] + list(range(1, chips, 2)) + [z for z in range(chips - 1, 0, -1) if z % 2 == 0]


def body(integrals, pair_lists, row_orbital, occ_energy, vir_energy):
    own_count, width, aux = integrals.shape
    slots = pair_lists.shape[1]
    groups = lax.axis_size("grp")
    me = lax.axis_index("grp")
    me_ref = me.astype(jnp.int32).reshape(1)
    chips = lax.axis_size("blk") // CORES
    order = ring_order(chips)
    ring = lambda s: [
        (order[i] * CORES + c, order[(i + s) % chips] * CORES + c) for i in range(chips) for c in range(CORES)
    ]
    swap = [(i, i ^ 1) for i in range(chips * CORES)]
    along = lambda x, s: lax.ppermute(x, "blk", ring(s))
    hop = lambda x: along(x, 1)
    sibling = lambda x: lax.ppermute(x, "blk", swap)
    to_group = lambda x, k: lax.ppermute(x, "grp", [(g, g ^ k) for g in range(groups)])

    packet = jnp.concatenate([pair_lists[0], row_orbital])
    packets = [packet] + [to_group(packet, k) for k in range(1, groups)]
    own_rows = integrals.reshape(own_count * width, aux)
    sib_rows = sibling(own_rows)

    part_width = width // PIECES
    blocks = [pick(me_ref, packets, slots, integrals, p * part_width, part_width) for p in range(PIECES)]

    own_half = split_rows(after(own_rows, *blocks[-1]))

    ids = lax.broadcasted_iota(jnp.int32, (groups, own_count, occ_energy.shape[0]), 2)
    orbitals = jnp.stack(packets)[:, slots:]
    row_energies = jnp.sum(jnp.where(orbitals[:, :, None] == ids, occ_energy, 0.0), axis=2)
    held_rows = lax.bitwise_xor(lax.broadcasted_iota(jnp.int32, (groups, own_count), 0), me) * own_count
    held_rows = held_rows + lax.broadcasted_iota(jnp.int32, (groups, own_count), 1)
    listed_here = pair_lists[0][:, None, None] == held_rows
    partner_energy = jnp.sum(jnp.where(listed_here, row_energies, 0.0), axis=(1, 2))
    sib_virtual = sibling(vir_energy)
    row_energy = row_energies[0][None, :, None] - jnp.stack([vir_energy, sib_virtual])[:, None, :]
    row_energy = row_energy.reshape(1, CORES * own_count * width)
    virtual = [vir_energy] + [along(vir_energy, s) for s in range(1, chips)]
    early_energies = [sib_virtual] + virtual[1:]
    virtual = jnp.stack(virtual)
    col_energy = partner_energy[None, None, :, None] - virtual.reshape(chips, PIECES, 1, part_width)
    col_energy = list(col_energy.reshape(chips, slots * width, 1))

    pieces = []
    for p in range(PIECES):
        sent = blocks[p]
        got = [to_group(block, k + 1) for k, block in enumerate(sent)]
        if p == 1:
            halves = (own_half, split_rows(after(sib_rows, pieces[0][0])))
        got = after(got, halves, pieces[-1][0]) if p else after(got, own_half, early_energies)
        part = choose(me_ref, packet, slots, integrals, got, p * part_width)
        pieces.append([part, hop(part)])
        if p == 1:
            pieces[0][1] = after(pieces[0][1], halves)
    parts = [piece[0] for piece in pieces]
    first = [piece[1] for piece in pieces]

    units = []
    grads = []
    for s in range(chips):
        if s == 1:
            parts = first
        elif s:
            parts = [hop(x) for x in parts]
        ready = list(parts)
        if s == 0:
            ready[1] = after(ready[1], first[0])
        if s == 1:
            ready = after(ready, *grads[0])
        if s == chips - 1:
            totals = [hop(after(grad, parts[0], *grads[-1])) for grad in grads[1]]
        one, grad = unit(halves, row_energy, col_energy[s], ready)
        units.append(one)
        grads.append(grad)
    rows = own_count * width
    step = block_rows(rows, 256)
    last = rows - step
    middle = 0
    last = rows // 2
    cuts = [(0, last), (last, rows)]
    aside = []
    for s in range(2, chips + 1):
        done = totals
        if s == 2:
            totals[0] = after(totals[0], *grads[-1])
        totals = [x + y for x, y in zip(totals, grads[s % chips])]
        if s == 2:
            aside.append(forward(after(units, *done), rows, last, []))
        if s == chips - 1:
            most = forward(after(units, done[0], aside[0]), rows + last, rows - last, [], partial=True)
            aside.append(complete(after(units[-1], most, *done), rows + last, most))
        if s < chips:
            totals = [hop(x) for x in totals]

    early = forward(after(units[:-1], aside[1]), 0, rows, [])
    known = [(0, early)] + [(begin, sibling(x)) for (begin, _), x in zip(cuts, aside)]
    density = forward(units[-1:], 0, rows, known).reshape(own_count, width, aux)
    arrived = []
    for p in range(PIECES):
        share = after(totals[p], known, *(arrived[-1] if p else []))
        sent = back(me_ref, packet, slots, own_count, share, groups)
        arrived.append([to_group(block, k + 1) for k, block in enumerate(sent)])
    return finish(me_ref, packets, slots, totals, arrived, density)


def solution(mesh):
    in_specs = (P("grp", "blk", None), P("grp", None), P("grp"), P(), P("blk"))
    out_specs = P("grp", "blk", None)
    return jax.shard_map(body, mesh=mesh, in_specs=in_specs, out_specs=out_specs, check_vma=False)
```

```python
import functools
import math

import jax
import jax.numpy as jnp
from jax import lax
from jax.experimental import pallas as pl
from jax.experimental.pallas import tpu as pltpu
from jax.sharding import PartitionSpec as P

PIECES = 2
CORES = 2
SCALE = 1
VMEM = 56 * 1024 * 1024
ANY = pl.BlockSpec(memory_space=pl.ANY)
SMEM = pl.BlockSpec(memory_space=pltpu.SMEM)
LOCAL = pl.BlockSpec(memory_space=pltpu.VMEM)
PARAMS = pltpu.CompilerParams(vmem_limit_bytes=VMEM)


def split(x):
    high = x.astype(jnp.bfloat16)
    return high, (x - high.astype(jnp.float32)).astype(jnp.bfloat16)


def dot(a, b, contract):
    return lax.dot_general(a, b, ((contract[:1], contract[1:]), ((), ())), preferred_element_type=jnp.float32)


def block_rows(total, most):
    rows = most
    while total % rows:
        rows //= 2
    return rows


def after(x, *others):
    return lax.optimization_barrier((x, others))[0]


def cost(flops, moved):
    return pl.CostEstimate(flops=flops // SCALE, bytes_accessed=moved // SCALE, transcendentals=0)


def split_kernel(x_ref, high_ref, low_ref):
    high_ref[...], low_ref[...] = split(x_ref[...])


def split_rows(x):
    rows, width = x.shape
    step = block_rows(rows, 256)
    spec = pl.BlockSpec((step, width), lambda i: (i, 0))
    half = jax.ShapeDtypeStruct(x.shape, jnp.bfloat16)
    return pl.pallas_call(
        split_kernel,
        grid=(rows // step,),
        in_specs=[spec],
        out_specs=[spec, spec],
        out_shape=[half, half],
        cost_estimate=cost(2 * rows * width, 8 * rows * width),
        compiler_params=PARAMS,
    )(x)


def asked_row(lists, me, slots, own_count):
    asked, row = False, 0
    for s in range(slots):
        entry = lists[s]
        hit = lax.div(entry, own_count) == me
        asked = jnp.logical_or(asked, hit)
        row = jnp.where(hit, entry - me * own_count, row)
    return asked, row


def slot_holder(lists, me, s, own_count):
    return lax.bitwise_xor(lax.div(lists[s], own_count), me)


def pick_kernel(groups, slots, own_count, first, me_ref, *refs):
    lists, x_ref, outs, sem = refs[:groups], refs[groups], refs[groups + 1:-1], refs[-1]
    rows = outs[0].shape[0]
    copies = []
    for k in range(1, groups):
        _, row = asked_row(lists[k], me_ref[0], slots, own_count)
        copies.append(pltpu.make_async_copy(x_ref.at[row, pl.ds(first, rows)], outs[k - 1], sem.at[k - 1]))
        copies[-1].start()
    for copy in copies:
        copy.wait()


def pick(me, lists, slots, integrals, first, rows):
    own_count, _, aux = integrals.shape
    groups = len(lists)
    return pl.pallas_call(
        functools.partial(pick_kernel, groups, slots, own_count, first),
        in_specs=[SMEM] * (groups + 1) + [ANY],
        out_specs=[LOCAL] * (groups - 1),
        out_shape=[jax.ShapeDtypeStruct((rows, aux), jnp.float32)] * (groups - 1),
        scratch_shapes=[pltpu.SemaphoreType.DMA((groups - 1,))],
        cost_estimate=cost(0, 8 * rows * aux * groups),
        compiler_params=PARAMS,
    )(me, *lists, integrals)


def choose_kernel(groups, slots, own_count, first, me_ref, lists, x_ref, *refs):
    got, out, sem = refs[:groups - 1], refs[groups - 1], refs[groups]
    rows = out.shape[0] // slots
    me = me_ref[0]
    for s in range(slots):
        k_of = slot_holder(lists, me, s, own_count)
        to = out.at[pl.ds(s * rows, rows)]
        row = jnp.clip(lists[s] - me * own_count, 0, own_count - 1)

        @pl.when(k_of == 0)
        def _():
            pltpu.make_async_copy(x_ref.at[row, pl.ds(first, rows)], to, sem.at[s]).start()

        for k in range(1, groups):
            @pl.when(k_of == k)
            def _():
                pltpu.make_async_copy(got[k - 1], to, sem.at[s]).start()

        @pl.when(k_of >= groups)
        def _():
            to[...] = jnp.zeros_like(to)

    for s in range(slots):
        @pl.when(slot_holder(lists, me, s, own_count) < groups)
        def _():
            pltpu.make_async_copy(got[0], out.at[pl.ds(s * rows, rows)], sem.at[s]).wait()


def choose(me, lists, slots, integrals, got, first):
    own_count, _, aux = integrals.shape
    rows = got[0].shape[0]
    groups = len(got) + 1
    return pl.pallas_call(
        functools.partial(choose_kernel, groups, slots, own_count, first),
        in_specs=[SMEM, SMEM] + [ANY] * groups,
        out_specs=LOCAL,
        out_shape=jax.ShapeDtypeStruct((slots * rows, aux), jnp.float32),
        scratch_shapes=[pltpu.SemaphoreType.DMA((slots,))],
        cost_estimate=cost(0, 8 * rows * aux * slots),
        compiler_params=PARAMS,
    )(me, lists, integrals, *got)


def back_kernel(groups, slots, own_count, me_ref, lists, share, *refs):
    outs, sem = refs[:-1], refs[-1]
    rows = outs[0].shape[0]
    copies = []
    for k in range(1, groups):
        slot = 0
        for s in range(slots):
            slot = jnp.where(slot_holder(lists, me_ref[0], s, own_count) == k, s, slot)
        start = pl.multiple_of(slot * rows, rows)
        copies.append(pltpu.make_async_copy(share.at[pl.ds(start, rows)], outs[k - 1], sem.at[k - 1]))
        copies[-1].start()
    for copy in copies:
        copy.wait()


def back(me, lists, slots, own_count, share, groups):
    rows, aux = share.shape[0] // slots, share.shape[1]
    return pl.pallas_call(
        functools.partial(back_kernel, groups, slots, own_count),
        in_specs=[SMEM, SMEM, ANY],
        out_specs=[LOCAL] * (groups - 1),
        out_shape=[jax.ShapeDtypeStruct((rows, aux), jnp.float32)] * (groups - 1),
        scratch_shapes=[pltpu.SemaphoreType.DMA((groups - 1,))],
        cost_estimate=cost(0, 8 * rows * aux * groups),
        compiler_params=PARAMS,
    )(me, lists, share)


def finish_kernel(groups, slots, own_count, me_ref, *refs):
    lists, refs = refs[:groups], refs[groups:]
    shares, refs = refs[:PIECES], refs[PIECES:]
    arrived = refs[:PIECES * (groups - 1)]
    _, density, held, added, sem_held, sem_added = refs[PIECES * (groups - 1):]
    rows = held.shape[1]
    me = me_ref[0]
    asked, places, heads = [], [], []
    for k in range(groups):
        is_asked, row = asked_row(lists[k], me, slots, own_count)
        head = k
        for j in range(k - 1, -1, -1):
            head = jnp.where(jnp.logical_and(asked[j], places[j] == row), j, head)
        asked.append(is_asked)
        places.append(row)
        heads.append(head)
    slot = 0
    for s in range(slots):
        slot = jnp.where(slot_holder(lists[0], me, s, own_count) == 0, s, slot)
    start = pl.multiple_of(slot * rows, rows)
    leads = [jnp.logical_and(asked[k], heads[k] == k) for k in range(groups)]
    every = [(p, k) for p in range(PIECES) for k in range(groups)]
    reads, terms, writes = {}, {}, {}
    for n, (p, k) in enumerate(every):
        source = arrived[p * (groups - 1) + k - 1] if k else shares[p].at[pl.ds(start, rows)]
        spot = density.at[places[k], pl.ds(p * rows, rows)]
        reads[p, k] = pltpu.make_async_copy(spot, held.at[n], sem_held.at[n])
        writes[p, k] = pltpu.make_async_copy(held.at[n], spot, sem_held.at[n])
        terms[p, k] = pltpu.make_async_copy(source, added.at[n], sem_added.at[n])
    for p, k in every:
        pl.when(leads[k])(reads[p, k].start)
        pl.when(asked[k])(terms[p, k].start)
    for p, k in every:
        pl.when(leads[k])(reads[p, k].wait)
    for n, (p, k) in enumerate(every):
        @pl.when(asked[k])
        def _():
            terms[p, k].wait()
            held[p * groups + heads[k]] = held[p * groups + heads[k]] + added[n]
    for p, k in every:
        pl.when(leads[k])(writes[p, k].start)
    for p, k in every:
        pl.when(leads[k])(writes[p, k].wait)


def finish(me, lists, slots, shares, arrived, density):
    own_count, _, aux = density.shape
    groups = len(lists)
    rows = shares[0].shape[0] // slots
    blocks = [block for piece in arrived for block in piece]
    operands = [me, *lists, *shares, *blocks, density]
    return pl.pallas_call(
        functools.partial(finish_kernel, groups, slots, own_count),
        in_specs=[SMEM] * (groups + 1) + [ANY] * (PIECES + len(blocks) + 1),
        out_specs=ANY,
        out_shape=jax.ShapeDtypeStruct(density.shape, jnp.float32),
        input_output_aliases={len(operands) - 1: 0},
        scratch_shapes=[pltpu.VMEM((PIECES * groups, rows, aux), jnp.float32)] * 2
        + [pltpu.SemaphoreType.DMA((PIECES * groups,))] * 2,
        cost_estimate=cost(0, 12 * rows * aux * groups * PIECES),
        compiler_params=PARAMS,
    )(*operands)


def unit_kernel(steps, own_high, own_low, sib_high, sib_low, row_ref, col_ref, *refs):
    parts = refs[:PIECES]
    t_high, t_low, r_high, r_low = refs[PIECES:PIECES + 4]
    grads = refs[PIECES + 4:2 * PIECES + 4]
    step = pl.program_id(0)
    width = parts[0].shape[0]

    @pl.when(step == 0)
    def _():
        for p in range(PIECES):
            part = slice(p * width, (p + 1) * width)
            r_high[part], r_low[part] = split(parts[p][...])
            grads[p][...] = jnp.zeros_like(grads[p])

    def work(a_high, a_low):
        high, low = r_high[...], r_low[...]
        pair = dot(high, a_high[...], (1, 1)) + dot(low, a_high[...], (1, 1)) + dot(high, a_low[...], (1, 1))
        up, down = split(pair / (row_ref[...] + col_ref[...]))
        t_high[...] = up
        t_low[...] = down
        term = dot(up, a_high[...], (1, 0)) + dot(down, a_high[...], (1, 0)) + dot(up, a_low[...], (1, 0))
        for p in range(PIECES):
            grads[p][...] += term[p * width:(p + 1) * width]

    @pl.when(step < steps)
    def _():
        work(own_high, own_low)

    @pl.when(step >= steps)
    def _():
        work(sib_high, sib_low)


def unit(halves, row_energy, col_energy, parts):
    (own_high, own_low), (sib_high, sib_low) = halves
    rows, aux = own_high.shape
    step = block_rows(rows, 512)
    steps = rows // step
    part_rows = parts[0].shape[0]
    cols = part_rows * PIECES
    own = pl.BlockSpec((step, aux), lambda i: (jnp.minimum(i, steps - 1), 0))
    sib = pl.BlockSpec((step, aux), lambda i: (jnp.maximum(i - steps, 0), 0))
    whole = lambda shape: pl.BlockSpec(shape, lambda i: (0, 0))
    bf16 = lambda *shape: jax.ShapeDtypeStruct(shape, jnp.bfloat16)
    t_spec = pl.BlockSpec((cols, step), lambda i: (0, i))
    outs = pl.pallas_call(
        functools.partial(unit_kernel, steps),
        grid=(2 * steps,),
        in_specs=[own, own, sib, sib, pl.BlockSpec((1, step), lambda i: (0, i)), whole((cols, 1))]
        + [whole((part_rows, aux))] * PIECES,
        out_specs=[t_spec, t_spec, whole((cols, aux)), whole((cols, aux))] + [whole((part_rows, aux))] * PIECES,
        out_shape=[bf16(cols, 2 * rows)] * 2 + [bf16(cols, aux)] * 2
        + [jax.ShapeDtypeStruct((part_rows, aux), jnp.float32)] * PIECES,
        cost_estimate=cost(24 * rows * aux * cols, 8 * rows * aux + 16 * cols * aux),
        compiler_params=PARAMS,
    )(own_high, own_low, sib_high, sib_low, row_energy, col_energy, *parts)
    return outs[:4], outs[4:]


def forward_term(refs):
    t_high, t_low, r_high, r_low = (ref[...] for ref in refs)
    return dot(t_high, r_high, (0, 0)) + dot(t_high, r_low, (0, 0)) + dot(t_low, r_high, (0, 0))


def forward_kernel(count, spans, partial, *refs):
    out = refs[-1]
    total = None
    for u in range(count - partial):
        term = forward_term(refs[4 * u:4 * u + 4])
        total = term if total is None else total + term
    out[...] = total
    step = pl.program_id(0)
    if partial:
        @pl.when(step < pl.num_programs(0) - 1)
        def _():
            out[...] += forward_term(refs[4 * (count - 1):4 * count])
    for (begin, end), start in zip(spans, refs[4 * count:-1]):
        @pl.when(jnp.logical_and(step >= begin, step < end))
        def _():
            out[...] += start[...]


def forward(units, first, count, starts, partial=False):
    cols, aux = units[0][2].shape
    step = block_rows(math.gcd(count, *(begin for begin, _ in starts), *(rows.shape[0] for _, rows in starts)), 256)
    steps = count // step
    spans = [(begin // step, (begin + rows.shape[0]) // step) for begin, rows in starts]
    t_spec = pl.BlockSpec((cols, step), lambda i: (0, i + first // step))
    r_spec = pl.BlockSpec((cols, aux), lambda i: (0, 0))
    out_spec = pl.BlockSpec((step, aux), lambda i: (i, 0))
    start_spec = lambda begin, end: pl.BlockSpec((step, aux), lambda i: (jnp.clip(i, begin, end - 1) - begin, 0))
    return pl.pallas_call(
        functools.partial(forward_kernel, len(units), spans, partial),
        grid=(steps,),
        in_specs=[t_spec, t_spec, r_spec, r_spec] * len(units) + [start_spec(*span) for span in spans],
        out_specs=out_spec,
        out_shape=jax.ShapeDtypeStruct((count, aux), jnp.float32),
        cost_estimate=cost(6 * count * aux * cols * len(units), 8 * count * aux),
        compiler_params=PARAMS,
    )(*(x for one in units for x in one), *(rows for _, rows in starts))


def complete_kernel(t_high, t_low, r_high, r_low, known, out):
    out[...] = known[...] + forward_term((t_high, t_low, r_high, r_low))


def complete(unit_parts, first, known):
    cols, aux = unit_parts[2].shape
    count = known.shape[0]
    step = block_rows(count, 256)
    last = count // step - 1
    t_spec = pl.BlockSpec((cols, step), lambda i: (0, first // step + last))
    r_spec = pl.BlockSpec((cols, aux), lambda i: (0, 0))
    block = pl.BlockSpec((step, aux), lambda i: (last, 0))
    return pl.pallas_call(
        complete_kernel,
        grid=(1,),
        in_specs=[t_spec, t_spec, r_spec, r_spec, block],
        out_specs=block,
        out_shape=jax.ShapeDtypeStruct(known.shape, jnp.float32),
        input_output_aliases={4: 0},
        cost_estimate=cost(6 * count * aux * cols, 8 * count * aux),
        compiler_params=PARAMS,
    )(*unit_parts, known)


def ring_order(chips):
    return [0] + list(range(1, chips, 2)) + [z for z in range(chips - 1, 0, -1) if z % 2 == 0]


def body(integrals, pair_lists, row_orbital, occ_energy, vir_energy):
    own_count, width, aux = integrals.shape
    slots = pair_lists.shape[1]
    groups = lax.axis_size("grp")
    me = lax.axis_index("grp")
    me_ref = me.astype(jnp.int32).reshape(1)
    chips = lax.axis_size("blk") // CORES
    order = ring_order(chips)
    ring = lambda s: [
        (order[i] * CORES + c, order[(i + s) % chips] * CORES + c) for i in range(chips) for c in range(CORES)
    ]
    swap = [(i, i ^ 1) for i in range(chips * CORES)]
    along = lambda x, s: lax.ppermute(x, "blk", ring(s))
    hop = lambda x: along(x, 1)
    sibling = lambda x: lax.ppermute(x, "blk", swap)
    to_group = lambda x, k: lax.ppermute(x, "grp", [(g, g ^ k) for g in range(groups)])

    packet = jnp.concatenate([pair_lists[0], row_orbital])
    packets = [packet] + [to_group(packet, k) for k in range(1, groups)]
    own_rows = integrals.reshape(own_count * width, aux)
    sib_rows = sibling(own_rows)

    part_width = width // PIECES
    blocks = [pick(me_ref, packets, slots, integrals, p * part_width, part_width) for p in range(PIECES)]

    ids = lax.broadcasted_iota(jnp.int32, (groups, own_count, occ_energy.shape[0]), 2)
    orbitals = jnp.stack(packets)[:, slots:]
    row_energies = jnp.sum(jnp.where(orbitals[:, :, None] == ids, occ_energy, 0.0), axis=2)
    held_rows = lax.bitwise_xor(lax.broadcasted_iota(jnp.int32, (groups, own_count), 0), me) * own_count
    held_rows = held_rows + lax.broadcasted_iota(jnp.int32, (groups, own_count), 1)
    listed_here = pair_lists[0][:, None, None] == held_rows
    partner_energy = jnp.sum(jnp.where(listed_here, row_energies, 0.0), axis=(1, 2))
    sib_virtual = sibling(vir_energy)
    row_energy = row_energies[0][None, :, None] - jnp.stack([vir_energy, sib_virtual])[:, None, :]
    row_energy = row_energy.reshape(1, CORES * own_count * width)
    virtual = [vir_energy] + [along(vir_energy, s) for s in range(1, chips)]
    early_energies = [sib_virtual] + virtual[1:]
    virtual = jnp.stack(virtual)
    col_energy = partner_energy[None, None, :, None] - virtual.reshape(chips, PIECES, 1, part_width)
    col_energy = list(col_energy.reshape(chips, slots * width, 1))

    pieces = []
    for p in range(PIECES):
        sent = blocks[p]
        got = [to_group(block, k + 1) for k, block in enumerate(sent)]
        if p == 1:
            own_half = split_rows(after(own_rows, pieces[0][0]))
        got = after(got, own_half, sib_rows, pieces[-1][0]) if p else after(got, early_energies)
        part = choose(me_ref, packet, slots, integrals, got, p * part_width)
        pieces.append([part, hop(part)])
    halves = (own_half, split_rows(after(sib_rows, pieces[1][0])))
    pieces[0][1] = after(pieces[0][1], halves)
    parts = [piece[0] for piece in pieces]
    first = [piece[1] for piece in pieces]

    units = []
    grads = []
    for s in range(chips):
        if s == 1:
            parts = first
        elif s:
            parts = [hop(x) for x in parts]
        ready = list(parts)
        if s == 0:
            ready[1] = after(ready[1], first[0])
        if s == 1:
            ready = after(ready, *grads[0])
        if s == chips - 1:
            totals = [hop(after(grad, parts[0], *grads[-1])) for grad in grads[1]]
        one, grad = unit(halves, row_energy, col_energy[s], ready)
        units.append(one)
        grads.append(grad)
    rows = own_count * width
    step = block_rows(rows, 256)
    last = rows - step
    middle = 0
    last = rows // 2
    cuts = [(0, last), (last, rows)]
    aside = []
    for s in range(2, chips + 1):
        done = totals
        if s == 2:
            totals[0] = after(totals[0], *grads[-1])
        totals = [x + y for x, y in zip(totals, grads[s % chips])]
        if s == 2:
            aside.append(forward(after(units, *done), rows, last, []))
        if s == chips - 1:
            most = forward(after(units, done[0], aside[0]), rows + last, rows - last, [], partial=True)
            aside.append(complete(after(units[-1], most, *done), rows + last, most))
        if s < chips:
            totals = [hop(x) for x in totals]

    early = forward(after(units[:-1], aside[1]), 0, rows, [])
    known = [(0, early)] + [(begin, sibling(x)) for (begin, _), x in zip(cuts, aside)]
    density = forward(units[-1:], 0, rows, known).reshape(own_count, width, aux)
    arrived = []
    for p in range(PIECES):
        share = after(totals[p], known, *(arrived[-1] if p else []))
        sent = back(me_ref, packet, slots, own_count, share, groups)
        arrived.append([to_group(block, k + 1) for k, block in enumerate(sent)])
    return finish(me_ref, packets, slots, totals, arrived, density)


def solution(mesh):
    in_specs = (P("grp", "blk", None), P("grp", None), P("grp"), P(), P("blk"))
    out_specs = P("grp", "blk", None)
    return jax.shard_map(body, mesh=mesh, in_specs=in_specs, out_specs=out_specs, check_vma=False)
```

```python
import functools
import math

import jax
import jax.numpy as jnp
from jax import lax
from jax.experimental import pallas as pl
from jax.experimental.pallas import tpu as pltpu
from jax.sharding import PartitionSpec as P

PIECES = 2
CORES = 2
SCALE = 1
VMEM = 56 * 1024 * 1024
ANY = pl.BlockSpec(memory_space=pl.ANY)
SMEM = pl.BlockSpec(memory_space=pltpu.SMEM)
LOCAL = pl.BlockSpec(memory_space=pltpu.VMEM)
PARAMS = pltpu.CompilerParams(vmem_limit_bytes=VMEM)


def split(x):
    high = x.astype(jnp.bfloat16)
    return high, (x - high.astype(jnp.float32)).astype(jnp.bfloat16)


def dot(a, b, contract):
    return lax.dot_general(a, b, ((contract[:1], contract[1:]), ((), ())), preferred_element_type=jnp.float32)


def block_rows(total, most):
    rows = most
    while total % rows:
        rows //= 2
    return rows


def after(x, *others):
    return lax.optimization_barrier((x, others))[0]


def cost(flops, moved):
    return pl.CostEstimate(flops=flops // SCALE, bytes_accessed=moved // SCALE, transcendentals=0)


def split_kernel(x_ref, high_ref, low_ref):
    high_ref[...], low_ref[...] = split(x_ref[...])


def split_rows(x):
    rows, width = x.shape
    step = block_rows(rows, 256)
    spec = pl.BlockSpec((step, width), lambda i: (i, 0))
    half = jax.ShapeDtypeStruct(x.shape, jnp.bfloat16)
    return pl.pallas_call(
        split_kernel,
        grid=(rows // step,),
        in_specs=[spec],
        out_specs=[spec, spec],
        out_shape=[half, half],
        cost_estimate=cost(2 * rows * width, 8 * rows * width),
        compiler_params=PARAMS,
    )(x)


def asked_row(lists, me, slots, own_count):
    asked, row = False, 0
    for s in range(slots):
        entry = lists[s]
        hit = lax.div(entry, own_count) == me
        asked = jnp.logical_or(asked, hit)
        row = jnp.where(hit, entry - me * own_count, row)
    return asked, row


def slot_holder(lists, me, s, own_count):
    return lax.bitwise_xor(lax.div(lists[s], own_count), me)


def pick_kernel(groups, slots, own_count, first, me_ref, *refs):
    lists, x_ref, outs, (held, sem, sent) = refs[:groups], refs[groups], refs[groups + 1:-3], refs[-3:]
    rows = outs[0].shape[0]
    copies = []
    for k in range(1, groups):
        _, row = asked_row(lists[k], me_ref[0], slots, own_count)
        copies.append(pltpu.make_async_copy(x_ref.at[row, pl.ds(first, rows)], held.at[k - 1], sem.at[k - 1]))
        copies[-1].start()
    leaving = [pltpu.make_async_copy(held.at[n], out, sent.at[n]) for n, out in enumerate(outs)]
    for copy, leave in zip(copies, leaving):
        copy.wait()
        leave.start()
    for leave in leaving:
        leave.wait()


def pick(me, lists, slots, integrals, first, rows):
    own_count, _, aux = integrals.shape
    groups = len(lists)
    return pl.pallas_call(
        functools.partial(pick_kernel, groups, slots, own_count, first),
        in_specs=[SMEM] * (groups + 1) + [ANY],
        out_specs=[ANY] * (groups - 1),
        out_shape=[jax.ShapeDtypeStruct((rows, aux), jnp.float32)] * (groups - 1),
        scratch_shapes=[pltpu.VMEM((groups - 1, rows, aux), jnp.float32)]
        + [pltpu.SemaphoreType.DMA((groups - 1,))] * 2,
        cost_estimate=cost(0, 8 * rows * aux * groups),
        compiler_params=PARAMS,
    )(me, *lists, integrals)


def choose_kernel(groups, slots, own_count, first, me_ref, lists, x_ref, *refs):
    got, out, sem = refs[:groups - 1], refs[groups - 1], refs[groups]
    rows = out.shape[0] // slots
    me = me_ref[0]
    for s in range(slots):
        k_of = slot_holder(lists, me, s, own_count)
        to = out.at[pl.ds(s * rows, rows)]
        row = jnp.clip(lists[s] - me * own_count, 0, own_count - 1)

        @pl.when(k_of == 0)
        def _():
            pltpu.make_async_copy(x_ref.at[row, pl.ds(first, rows)], to, sem.at[s]).start()

        for k in range(1, groups):
            @pl.when(k_of == k)
            def _():
                pltpu.make_async_copy(got[k - 1], to, sem.at[s]).start()

        @pl.when(k_of >= groups)
        def _():
            to[...] = jnp.zeros_like(to)

    for s in range(slots):
        @pl.when(slot_holder(lists, me, s, own_count) < groups)
        def _():
            pltpu.make_async_copy(got[0], out.at[pl.ds(s * rows, rows)], sem.at[s]).wait()


def choose(me, lists, slots, integrals, got, first):
    own_count, _, aux = integrals.shape
    rows = got[0].shape[0]
    groups = len(got) + 1
    return pl.pallas_call(
        functools.partial(choose_kernel, groups, slots, own_count, first),
        in_specs=[SMEM, SMEM] + [ANY] * groups,
        out_specs=LOCAL,
        out_shape=jax.ShapeDtypeStruct((slots * rows, aux), jnp.float32),
        scratch_shapes=[pltpu.SemaphoreType.DMA((slots,))],
        cost_estimate=cost(0, 8 * rows * aux * slots),
        compiler_params=PARAMS,
    )(me, lists, integrals, *got)


def back_kernel(groups, slots, own_count, me_ref, lists, share, *refs):
    outs, (held, sem, sent) = refs[:-3], refs[-3:]
    rows = outs[0].shape[0]
    copies = []
    for k in range(1, groups):
        slot = 0
        for s in range(slots):
            slot = jnp.where(slot_holder(lists, me_ref[0], s, own_count) == k, s, slot)
        start = pl.multiple_of(slot * rows, rows)
        copies.append(pltpu.make_async_copy(share.at[pl.ds(start, rows)], held.at[k - 1], sem.at[k - 1]))
        copies[-1].start()
    leaving = [pltpu.make_async_copy(held.at[n], out, sent.at[n]) for n, out in enumerate(outs)]
    for copy, leave in zip(copies, leaving):
        copy.wait()
        leave.start()
    for leave in leaving:
        leave.wait()


def back(me, lists, slots, own_count, share, groups):
    rows, aux = share.shape[0] // slots, share.shape[1]
    return pl.pallas_call(
        functools.partial(back_kernel, groups, slots, own_count),
        in_specs=[SMEM, SMEM, ANY],
        out_specs=[ANY] * (groups - 1),
        out_shape=[jax.ShapeDtypeStruct((rows, aux), jnp.float32)] * (groups - 1),
        scratch_shapes=[pltpu.VMEM((groups - 1, rows, aux), jnp.float32)]
        + [pltpu.SemaphoreType.DMA((groups - 1,))] * 2,
        cost_estimate=cost(0, 8 * rows * aux * groups),
        compiler_params=PARAMS,
    )(me, lists, share)


def finish_kernel(groups, slots, own_count, me_ref, *refs):
    lists, refs = refs[:groups], refs[groups:]
    shares, refs = refs[:PIECES], refs[PIECES:]
    arrived = refs[:PIECES * (groups - 1)]
    _, density, held, added, sem_held, sem_added = refs[PIECES * (groups - 1):]
    rows = held.shape[1]
    me = me_ref[0]
    asked, places, heads = [], [], []
    for k in range(groups):
        is_asked, row = asked_row(lists[k], me, slots, own_count)
        head = k
        for j in range(k - 1, -1, -1):
            head = jnp.where(jnp.logical_and(asked[j], places[j] == row), j, head)
        asked.append(is_asked)
        places.append(row)
        heads.append(head)
    slot = 0
    for s in range(slots):
        slot = jnp.where(slot_holder(lists[0], me, s, own_count) == 0, s, slot)
    start = pl.multiple_of(slot * rows, rows)
    leads = [jnp.logical_and(asked[k], heads[k] == k) for k in range(groups)]
    every = [(p, k) for p in range(PIECES) for k in range(groups)]
    reads, terms, writes = {}, {}, {}
    for n, (p, k) in enumerate(every):
        source = arrived[p * (groups - 1) + k - 1] if k else shares[p].at[pl.ds(start, rows)]
        spot = density.at[places[k], pl.ds(p * rows, rows)]
        reads[p, k] = pltpu.make_async_copy(spot, held.at[n], sem_held.at[n])
        writes[p, k] = pltpu.make_async_copy(held.at[n], spot, sem_held.at[n])
        terms[p, k] = pltpu.make_async_copy(source, added.at[n], sem_added.at[n])
    for p, k in every:
        pl.when(leads[k])(reads[p, k].start)
        pl.when(asked[k])(terms[p, k].start)
    for p, k in every:
        pl.when(leads[k])(reads[p, k].wait)
    for n, (p, k) in enumerate(every):
        @pl.when(asked[k])
        def _():
            terms[p, k].wait()
            held[p * groups + heads[k]] = held[p * groups + heads[k]] + added[n]
    for p, k in every:
        pl.when(leads[k])(writes[p, k].start)
    for p, k in every:
        pl.when(leads[k])(writes[p, k].wait)


def finish(me, lists, slots, shares, arrived, density):
    own_count, _, aux = density.shape
    groups = len(lists)
    rows = shares[0].shape[0] // slots
    blocks = [block for piece in arrived for block in piece]
    operands = [me, *lists, *shares, *blocks, density]
    return pl.pallas_call(
        functools.partial(finish_kernel, groups, slots, own_count),
        in_specs=[SMEM] * (groups + 1) + [ANY] * (PIECES + len(blocks) + 1),
        out_specs=ANY,
        out_shape=jax.ShapeDtypeStruct(density.shape, jnp.float32),
        input_output_aliases={len(operands) - 1: 0},
        scratch_shapes=[pltpu.VMEM((PIECES * groups, rows, aux), jnp.float32)] * 2
        + [pltpu.SemaphoreType.DMA((PIECES * groups,))] * 2,
        cost_estimate=cost(0, 12 * rows * aux * groups * PIECES),
        compiler_params=PARAMS,
    )(*operands)


def unit_kernel(steps, own_high, own_low, sib_high, sib_low, row_ref, col_ref, *refs):
    parts = refs[:PIECES]
    t_high, t_low, r_high, r_low = refs[PIECES:PIECES + 4]
    grads = refs[PIECES + 4:2 * PIECES + 4]
    step = pl.program_id(0)
    width = parts[0].shape[0]

    @pl.when(step == 0)
    def _():
        for p in range(PIECES):
            part = slice(p * width, (p + 1) * width)
            r_high[part], r_low[part] = split(parts[p][...])
            grads[p][...] = jnp.zeros_like(grads[p])

    def work(a_high, a_low):
        high, low = r_high[...], r_low[...]
        pair = dot(high, a_high[...], (1, 1)) + dot(low, a_high[...], (1, 1)) + dot(high, a_low[...], (1, 1))
        up, down = split(pair / (row_ref[...] + col_ref[...]))
        t_high[...] = up
        t_low[...] = down
        term = dot(up, a_high[...], (1, 0)) + dot(down, a_high[...], (1, 0)) + dot(up, a_low[...], (1, 0))
        for p in range(PIECES):
            grads[p][...] += term[p * width:(p + 1) * width]

    @pl.when(step < steps)
    def _():
        work(own_high, own_low)

    @pl.when(step >= steps)
    def _():
        work(sib_high, sib_low)


def unit(halves, row_energy, col_energy, parts):
    (own_high, own_low), (sib_high, sib_low) = halves
    rows, aux = own_high.shape
    step = block_rows(rows, 512)
    steps = rows // step
    part_rows = parts[0].shape[0]
    cols = part_rows * PIECES
    own = pl.BlockSpec((step, aux), lambda i: (jnp.minimum(i, steps - 1), 0))
    sib = pl.BlockSpec((step, aux), lambda i: (jnp.maximum(i - steps, 0), 0))
    whole = lambda shape: pl.BlockSpec(shape, lambda i: (0, 0))
    bf16 = lambda *shape: jax.ShapeDtypeStruct(shape, jnp.bfloat16)
    t_spec = pl.BlockSpec((cols, step), lambda i: (0, i))
    outs = pl.pallas_call(
        functools.partial(unit_kernel, steps),
        grid=(2 * steps,),
        in_specs=[own, own, sib, sib, pl.BlockSpec((1, step), lambda i: (0, i)), whole((cols, 1))]
        + [whole((part_rows, aux))] * PIECES,
        out_specs=[t_spec, t_spec, whole((cols, aux)), whole((cols, aux))] + [whole((part_rows, aux))] * PIECES,
        out_shape=[bf16(cols, 2 * rows)] * 2 + [bf16(cols, aux)] * 2
        + [jax.ShapeDtypeStruct((part_rows, aux), jnp.float32)] * PIECES,
        cost_estimate=cost(24 * rows * aux * cols, 8 * rows * aux + 16 * cols * aux),
        compiler_params=PARAMS,
    )(own_high, own_low, sib_high, sib_low, row_energy, col_energy, *parts)
    return outs[:4], outs[4:]


def forward_term(refs):
    t_high, t_low, r_high, r_low = (ref[...] for ref in refs)
    return dot(t_high, r_high, (0, 0)) + dot(t_high, r_low, (0, 0)) + dot(t_low, r_high, (0, 0))


def forward_kernel(count, spans, partial, *refs):
    out = refs[-1]
    total = None
    for u in range(count - partial):
        term = forward_term(refs[4 * u:4 * u + 4])
        total = term if total is None else total + term
    out[...] = total
    step = pl.program_id(0)
    if partial:
        @pl.when(step < pl.num_programs(0) - 1)
        def _():
            out[...] += forward_term(refs[4 * (count - 1):4 * count])
    for (begin, end), start in zip(spans, refs[4 * count:-1]):
        @pl.when(jnp.logical_and(step >= begin, step < end))
        def _():
            out[...] += start[...]


def forward(units, first, count, starts, partial=False):
    cols, aux = units[0][2].shape
    step = block_rows(math.gcd(count, *(begin for begin, _ in starts), *(rows.shape[0] for _, rows in starts)), 256)
    steps = count // step
    spans = [(begin // step, (begin + rows.shape[0]) // step) for begin, rows in starts]
    t_spec = pl.BlockSpec((cols, step), lambda i: (0, i + first // step))
    r_spec = pl.BlockSpec((cols, aux), lambda i: (0, 0))
    out_spec = pl.BlockSpec((step, aux), lambda i: (i, 0))
    start_spec = lambda begin, end: pl.BlockSpec((step, aux), lambda i: (jnp.clip(i, begin, end - 1) - begin, 0))
    return pl.pallas_call(
        functools.partial(forward_kernel, len(units), spans, partial),
        grid=(steps,),
        in_specs=[t_spec, t_spec, r_spec, r_spec] * len(units) + [start_spec(*span) for span in spans],
        out_specs=out_spec,
        out_shape=jax.ShapeDtypeStruct((count, aux), jnp.float32),
        cost_estimate=cost(6 * count * aux * cols * len(units), 8 * count * aux),
        compiler_params=PARAMS,
    )(*(x for one in units for x in one), *(rows for _, rows in starts))


def complete_kernel(t_high, t_low, r_high, r_low, known, out):
    out[...] = known[...] + forward_term((t_high, t_low, r_high, r_low))


def complete(unit_parts, first, known):
    cols, aux = unit_parts[2].shape
    count = known.shape[0]
    step = block_rows(count, 256)
    last = count // step - 1
    t_spec = pl.BlockSpec((cols, step), lambda i: (0, first // step + last))
    r_spec = pl.BlockSpec((cols, aux), lambda i: (0, 0))
    block = pl.BlockSpec((step, aux), lambda i: (last, 0))
    return pl.pallas_call(
        complete_kernel,
        grid=(1,),
        in_specs=[t_spec, t_spec, r_spec, r_spec, block],
        out_specs=block,
        out_shape=jax.ShapeDtypeStruct(known.shape, jnp.float32),
        input_output_aliases={4: 0},
        cost_estimate=cost(6 * count * aux * cols, 8 * count * aux),
        compiler_params=PARAMS,
    )(*unit_parts, known)


def ring_order(chips):
    return [0] + list(range(1, chips, 2)) + [z for z in range(chips - 1, 0, -1) if z % 2 == 0]


def body(integrals, pair_lists, row_orbital, occ_energy, vir_energy):
    own_count, width, aux = integrals.shape
    slots = pair_lists.shape[1]
    groups = lax.axis_size("grp")
    me = lax.axis_index("grp")
    me_ref = me.astype(jnp.int32).reshape(1)
    chips = lax.axis_size("blk") // CORES
    order = ring_order(chips)
    ring = lambda s: [
        (order[i] * CORES + c, order[(i + s) % chips] * CORES + c) for i in range(chips) for c in range(CORES)
    ]
    swap = [(i, i ^ 1) for i in range(chips * CORES)]
    along = lambda x, s: lax.ppermute(x, "blk", ring(s))
    hop = lambda x: along(x, 1)
    sibling = lambda x: lax.ppermute(x, "blk", swap)
    to_group = lambda x, k: lax.ppermute(x, "grp", [(g, g ^ k) for g in range(groups)])

    packet = jnp.concatenate([pair_lists[0], row_orbital])
    packets = [packet] + [to_group(packet, k) for k in range(1, groups)]
    own_rows = integrals.reshape(own_count * width, aux)
    sib_rows = sibling(own_rows)

    part_width = width // PIECES
    blocks = [pick(me_ref, packets, slots, integrals, p * part_width, part_width) for p in range(PIECES)]

    ids = lax.broadcasted_iota(jnp.int32, (groups, own_count, occ_energy.shape[0]), 2)
    orbitals = jnp.stack(packets)[:, slots:]
    row_energies = jnp.sum(jnp.where(orbitals[:, :, None] == ids, occ_energy, 0.0), axis=2)
    held_rows = lax.bitwise_xor(lax.broadcasted_iota(jnp.int32, (groups, own_count), 0), me) * own_count
    held_rows = held_rows + lax.broadcasted_iota(jnp.int32, (groups, own_count), 1)
    listed_here = pair_lists[0][:, None, None] == held_rows
    partner_energy = jnp.sum(jnp.where(listed_here, row_energies, 0.0), axis=(1, 2))
    sib_virtual = sibling(vir_energy)
    row_energy = row_energies[0][None, :, None] - jnp.stack([vir_energy, sib_virtual])[:, None, :]
    row_energy = row_energy.reshape(1, CORES * own_count * width)
    virtual = [vir_energy] + [along(vir_energy, s) for s in range(1, chips)]
    early_energies = [sib_virtual] + virtual[1:]
    virtual = jnp.stack(virtual)
    col_energy = partner_energy[None, None, :, None] - virtual.reshape(chips, PIECES, 1, part_width)
    col_energy = list(col_energy.reshape(chips, slots * width, 1))

    pieces = []
    for p in range(PIECES):
        sent = blocks[p]
        got = [to_group(block, k + 1) for k, block in enumerate(sent)]
        if p == 1:
            own_half = split_rows(after(own_rows, pieces[0][0]))
        got = after(got, own_half, sib_rows, pieces[-1][0]) if p else after(got, early_energies)
        part = choose(me_ref, packet, slots, integrals, got, p * part_width)
        pieces.append([part, hop(part)])
    halves = (own_half, split_rows(after(sib_rows, pieces[1][0])))
    pieces[0][1] = after(pieces[0][1], halves)
    parts = [piece[0] for piece in pieces]
    first = [piece[1] for piece in pieces]

    units = []
    grads = []
    for s in range(chips):
        if s == 1:
            parts = first
        elif s:
            parts = [hop(x) for x in parts]
        ready = list(parts)
        if s == 0:
            ready[1] = after(ready[1], first[0])
        if s == 1:
            ready = after(ready, *grads[0])
        if s == chips - 1:
            totals = [hop(after(grad, parts[0], *grads[-1])) for grad in grads[1]]
        one, grad = unit(halves, row_energy, col_energy[s], ready)
        units.append(one)
        grads.append(grad)
    rows = own_count * width
    step = block_rows(rows, 256)
    last = rows - step
    middle = 0
    last = rows // 2
    cuts = [(0, last), (last, rows)]
    aside = []
    for s in range(2, chips + 1):
        done = totals
        if s == 2:
            totals[0] = after(totals[0], *grads[-1])
        totals = [x + y for x, y in zip(totals, grads[s % chips])]
        if s == 2:
            aside.append(forward(after(units, *done), rows, last, []))
        if s == chips - 1:
            most = forward(after(units, done[0], aside[0]), rows + last, rows - last, [], partial=True)
            aside.append(complete(after(units[-1], most, *done), rows + last, most))
        if s < chips:
            totals = [hop(x) for x in totals]

    early = forward(after(units[:-1], aside[1]), 0, rows, [])
    known = [(0, early)] + [(begin, sibling(x)) for (begin, _), x in zip(cuts, aside)]
    density = forward(units[-1:], 0, rows, known).reshape(own_count, width, aux)
    arrived = []
    for p in range(PIECES):
        share = after(totals[p], known, *(arrived[-1] if p else []))
        sent = back(me_ref, packet, slots, own_count, share, groups)
        arrived.append([to_group(block, k + 1) for k, block in enumerate(sent)])
    return finish(me_ref, packets, slots, totals, arrived, density)


def solution(mesh):
    in_specs = (P("grp", "blk", None), P("grp", None), P("grp"), P(), P("blk"))
    out_specs = P("grp", "blk", None)
    return jax.shard_map(body, mesh=mesh, in_specs=in_specs, out_specs=out_specs, check_vma=False)
```
